32 devices in a mesh: dp: 4 (over z), tensor: 8 (over y, x, core).
Axes of the slice: x: 2, y: 2, z: 4, core: 2. Of those that a mesh axis runs over, the one named last changes fastest.
Arguments:
- tokens: bfloat16 [256, 4096], P(('dp', 'tensor')), may hold values from -6 to 6
- out_grad: bfloat16 [256, 4096], P(('dp', 'tensor')), may hold values from -6 to 6
- gate_blocks: bfloat16 [1792, 128, 128], P('tensor'), may hold values from -0.125 to 0.125
- up_blocks: bfloat16 [1792, 128, 128], P('tensor'), may hold values from -0.125 to 0.125
- down_blocks: bfloat16 [1792, 128, 128], P('tensor'), may hold values from -0.0625 to 0.0625
- gate_index: int32 [8, 224], P('tensor'), may hold values from 0 to 447, as said below
- up_index: int32 [8, 224], P('tensor'), may hold values from 0 to 447, as said below
- down_index: int32 [8, 224], P('tensor'), may hold values from 0 to 447, as said below
- gate_slot: int32 [8, 224], P('tensor'), may hold values from 0 to 279, as said below
- up_slot: int32 [8, 224], P('tensor'), may hold values from 0 to 279, as said below
- down_slot: int32 [8, 224], P('tensor'), may hold values from 0 to 279, as said below
Outputs:
- layer_out: bfloat16 [256, 4096], P(('dp', 'tensor'))
- token_grad: bfloat16 [256, 4096], P(('dp', 'tensor'))
- gate_grad: float32 [8, 280, 128, 128], P('tensor', 'dp')
- up_grad: float32 [8, 280, 128, 128], P('tensor', 'dp')
- down_grad: float32 [8, 280, 128, 128], P('tensor', 'dp')
The draws below stay inside these ranges and needn't reach their ends.
Inputs may be any that keep to these rules, and one draw needn't show every extreme that they name: `gate_index`: each row holds 224 distinct block numbers in increasing order. `up_index`: each row holds 224 distinct block numbers in increasing order. `down_index`: each row holds 224 distinct block numbers in increasing order. `gate_slot`: each row's 224 values are distinct; value v is slot v % 70 of data group v // 70; in every row some data group receives exactly 70 blocks. `up_slot`: each row's 224 values are distinct; value v is slot v % 70 of data group v // 70; in every row some data group receives exactly 70 blocks. `down_slot`: each row's 224 values are distinct; value v is slot v % 70 of data group v // 70; in every row some data group receives exactly 70 blocks.
All inputs are finite; a program needn't handle non-finite values.
Results may differ from the reference program's by a relative error of at most 0.019.
Values may be sent and summed in bfloat16 or wider, within the bound.
No kernel may reach another device: no remote copies, remote signals or barrier semaphores. Data moves between devices by JAX's collectives and lax.ppermute only.
A program may use at most 192 MiB of HBM per device.

```python
import math
import jax
import jax.numpy as jnp
from jax import lax

D = 4096
FF = 14336
BLK = 128
GROUP_TOK = 64
TOKENS = 256
FF_DEV = 1792
NBLK = 448
KB = 224
CAP = 70
N_DP = 4
N_TENSOR = 8


def kept_lists(key):
    keys = jax.random.split(key, N_TENSOR)

    def one_row(row_key):
        order = jax.random.permutation(row_key, NBLK)
        return jnp.sort(order[:KB])
    return jax.vmap(one_row)(keys).astype(jnp.int32)


def slot_lists(key):
    keys = jax.random.split(key, N_TENSOR)
    slot_total = N_DP * CAP

    def one_row(row_key):
        first_key, second_key, third_key = jax.random.split(row_key, 3)
        fullest = jax.random.randint(first_key, (), 0, N_DP)
        ranks = jax.random.permutation(second_key, slot_total)
        slot_ids = jnp.arange(slot_total, dtype=jnp.int32)
        scores = jnp.where(slot_ids // CAP == fullest, ranks, ranks + slot_total)
        ordered = jnp.argsort(scores, stable=True)
        return jax.random.permutation(third_key, ordered[:KB])
    return jax.vmap(one_row)(keys).astype(jnp.int32)


def draw_gate_index(key, part):
    return kept_lists(jax.random.fold_in(key, 101))


def draw_up_index(key, part):
    return kept_lists(jax.random.fold_in(key, 202))


def draw_down_index(key, part):
    return kept_lists(jax.random.fold_in(key, 303))


def draw_gate_slot(key, part):
    return slot_lists(jax.random.fold_in(key, 404))


def draw_up_slot(key, part):
    return slot_lists(jax.random.fold_in(key, 505))


def draw_down_slot(key, part):
    return slot_lists(jax.random.fold_in(key, 606))


def shard_levels(rng, extent, cuts, least, top_value):
    def one(dim, parts):
        draws = jax.random.uniform(jax.random.fold_in(jax.random.fold_in(rng, 6), dim), (parts,), jnp.float32, least / len(cuts), top_value / len(cuts))
        return jnp.repeat(jnp.exp(draws), extent[dim] // parts).reshape((-1,) + (1,) * (len(extent) - dim - 1))

    gain = one(*cuts[0])
    for cut in cuts[1:]:
        gain = gain * one(*cut)
    return gain


def centred(own_key, shape, deviation, limit, pieces=(), kind=jnp.bfloat16):
    array = jax.random.normal(own_key, shape, jnp.float32) * deviation
    if len(pieces) > 0:
        array = shard_levels(own_key, shape, pieces, -0.22, 0.18) * array
    return jnp.clip(array, min=-limit, max=limit).astype(kind)


def setup_inputs(seed: int = 0) -> dict:
    arg_keys = jax.random.split(jax.random.key(seed), 12)
    return {
        "tokens": centred(arg_keys[0], (TOKENS, D), 1.0, 6.0, ((0, 32),)),
        "out_grad": centred(arg_keys[1], (TOKENS, D), 1.0, 6.0, ((0, 32),)),
        "gate_blocks": centred(arg_keys[2], (N_TENSOR * KB, BLK, BLK), (D // 2) ** -0.5, 0.125, ((0, 8),)),
        "up_blocks": centred(arg_keys[3], (N_TENSOR * KB, BLK, BLK), (D // 2) ** -0.5, 0.125, ((0, 8),)),
        "down_blocks": centred(arg_keys[4], (N_TENSOR * KB, BLK, BLK), (FF // 2) ** -0.5, 0.0625, ((0, 8),)),
        "gate_index": draw_gate_index(jax.random.fold_in(arg_keys[11], 71), 0),
        "up_index": draw_up_index(jax.random.fold_in(arg_keys[11], 71), 0),
        "down_index": draw_down_index(jax.random.fold_in(arg_keys[11], 71), 0),
        "gate_slot": draw_gate_slot(jax.random.fold_in(arg_keys[11], 71), 0),
        "up_slot": draw_up_slot(jax.random.fold_in(arg_keys[11], 71), 0),
        "down_slot": draw_down_slot(jax.random.fold_in(arg_keys[11], 71), 0),
    }


def rounded(value):
    return lax.optimization_barrier(value.astype(jnp.bfloat16)).astype(jnp.float32)

def col_sums(source, blocks, block_rows, block_cols, out_count):
    picked = jnp.take(source, block_rows, axis=1).astype(jnp.float32)
    product = jnp.einsum('tkd,kde->tke', picked, blocks.astype(jnp.float32), precision=lax.Precision.HIGHEST)
    onehot = (block_cols[:, None] == jnp.arange(out_count, dtype=jnp.int32)[None, :]).astype(jnp.float32)
    summed = jnp.einsum('tke,kc->tce', product, onehot, precision=lax.Precision.HIGHEST)
    return summed.reshape(summed.shape[0], out_count * blocks.shape[2])

def row_sums(source, blocks, block_rows, block_cols, out_count):
    picked = jnp.take(source, block_cols, axis=1).astype(jnp.float32)
    product = jnp.einsum('tke,kde->tkd', picked, blocks.astype(jnp.float32), precision=lax.Precision.HIGHEST)
    onehot = (block_rows[:, None] == jnp.arange(out_count, dtype=jnp.int32)[None, :]).astype(jnp.float32)
    summed = jnp.einsum('tkd,kr->trd', product, onehot, precision=lax.Precision.HIGHEST)
    return summed.reshape(summed.shape[0], out_count * blocks.shape[1])

def group_terms(left_side, right_side, block_rows, block_cols, factor):
    left_groups = left_side.reshape(N_DP, GROUP_TOK, left_side.shape[1], left_side.shape[2])
    right_groups = right_side.reshape(N_DP, GROUP_TOK, right_side.shape[1], right_side.shape[2])
    picked_left = jnp.take(left_groups, block_rows, axis=2).astype(jnp.float32)
    picked_right = jnp.take(right_groups, block_cols, axis=2).astype(jnp.float32)
    terms = jnp.einsum('gtkd,gtke->gkde', picked_left, picked_right, precision=lax.Precision.HIGHEST) * factor
    return lax.optimization_barrier(jnp.sum(rounded(terms), axis=0))

def reference(tokens, out_grad, gate_blocks, up_blocks, down_blocks, gate_index, up_index, down_index, gate_slot, up_slot, down_slot):
    ff_cols = FF_DEV // BLK
    d_cols = D // BLK
    token_blocks = tokens.reshape(TOKENS, d_cols, BLK)
    cot_blocks = out_grad.reshape(TOKENS, d_cols, BLK)
    factor = jnp.float32(1.0 / math.sqrt(TOKENS))

    def one_slice(carry, shard_id):
        out_acc, grad_acc = carry
        gate_part = lax.dynamic_slice_in_dim(gate_blocks, shard_id * KB, KB, 0)
        up_part = lax.dynamic_slice_in_dim(up_blocks, shard_id * KB, KB, 0)
        down_part = lax.dynamic_slice_in_dim(down_blocks, shard_id * KB, KB, 0)
        gate_ids = gate_index[shard_id]
        up_ids = up_index[shard_id]
        down_ids = down_index[shard_id]
        gate_rows, gate_cols = (gate_ids // ff_cols, gate_ids % ff_cols)
        up_rows, up_cols = (up_ids // ff_cols, up_ids % ff_cols)
        down_rows, down_cols = (down_ids // d_cols, down_ids % d_cols)
        gate_act = col_sums(token_blocks, gate_part, gate_rows, gate_cols, ff_cols)
        up_act = col_sums(token_blocks, up_part, up_rows, up_cols, ff_cols)
        sigma = jax.nn.sigmoid(gate_act)
        hidden = (gate_act * sigma * up_act).astype(jnp.bfloat16)
        hidden_blocks = hidden.reshape(TOKENS, ff_cols, BLK)
        down_partial = rounded(col_sums(hidden_blocks, down_part, down_rows, down_cols, d_cols))
        hidden_grad = row_sums(cot_blocks, down_part, down_rows, down_cols, ff_cols)
        gate_pre = (hidden_grad * up_act * sigma * (1.0 + gate_act * (1.0 - sigma))).astype(jnp.bfloat16)
        up_pre = (hidden_grad * gate_act * sigma).astype(jnp.bfloat16)
        gate_pre_blocks = gate_pre.reshape(TOKENS, ff_cols, BLK)
        up_pre_blocks = up_pre.reshape(TOKENS, ff_cols, BLK)
        input_partial = row_sums(gate_pre_blocks, gate_part, gate_rows, gate_cols, d_cols)
        input_partial = rounded(input_partial + row_sums(up_pre_blocks, up_part, up_rows, up_cols, d_cols))
        gate_sum = group_terms(token_blocks, gate_pre_blocks, gate_rows, gate_cols, factor)
        up_sum = group_terms(token_blocks, up_pre_blocks, up_rows, up_cols, factor)
        down_sum = group_terms(hidden_blocks, cot_blocks, down_rows, down_cols, factor)
        return ((out_acc + down_partial, grad_acc + input_partial), (gate_sum, up_sum, down_sum))
    start_acc = (jnp.zeros((TOKENS, D), jnp.float32), jnp.zeros((TOKENS, D), jnp.float32))
    (out_acc, grad_acc), (gate_all, up_all, down_all) = lax.scan(one_slice, start_acc, jnp.arange(N_TENSOR, dtype=jnp.int32))

    def place(slots, sums):
        return jnp.zeros((N_DP * CAP, BLK, BLK), jnp.float32).at[slots].set(sums)
    gate_grad = jax.vmap(place)(gate_slot, gate_all)
    up_grad = jax.vmap(place)(up_slot, up_all)
    down_grad = jax.vmap(place)(down_slot, down_all)
    return (out_acc.astype(jnp.bfloat16), grad_acc.astype(jnp.bfloat16), gate_grad, up_grad, down_grad)
```

```python
import functools
import math

import jax
import jax.numpy as jnp
from jax import lax
from jax.experimental import pallas as pl
from jax.experimental.pallas import tpu as pltpu
from jax.sharding import PartitionSpec as P

FF = 14336
BF16 = jnp.bfloat16
F32 = jnp.float32
VMEM = pltpu.VMEM
SMEM = pltpu.SMEM


def in_vmem():
    return pl.BlockSpec(memory_space=VMEM)


def pinned(*arrays):
    return [pltpu.with_memory_space_constraint(x, VMEM) for x in arrays]


def dot_nn(a, b):
    return lax.dot_general(a, b, (((1,), (0,)), ((), ())), preferred_element_type=F32)


def dot_nt(a, b):
    return lax.dot_general(a, b, (((1,), (1,)), ((), ())), preferred_element_type=F32)


def exchange(x, axis, flip):
    count = lax.axis_size(axis)
    return lax.ppermute(x, axis, [(i, i ^ flip) for i in range(count)])


def densify_body(gi, ui, di, gb, ub, db, wg, wu, wd, sem):
    kept = gb.shape[0]

    def fill(index, blocks, dense, slot):
        cols = dense.shape[1] // blocks.shape[2]
        size = blocks.shape[1]
        dense[...] = jnp.zeros_like(dense)

        def step(i, carry):
            for u in range(8):
                k = i * 8 + u
                b = index[0, k]
                r = pl.multiple_of((b // cols) * size, size)
                c = pl.multiple_of((b % cols) * size, size)
                pltpu.make_async_copy(
                    blocks.at[k], dense.at[pl.ds(r, size), pl.ds(c, size)], sem.at[slot]
                ).start()
            return carry

        lax.fori_loop(0, kept // 8, step, 0)

    fill(gi, gb, wg, 0)
    fill(ui, ub, wu, 1)
    fill(di, db, wd, 2)
    for slot, blocks in enumerate((gb, ub, db)):
        pltpu.make_async_copy(blocks, blocks, sem.at[slot]).wait()


def densify(gate_index, up_index, down_index, gate_blocks, up_blocks, down_blocks, width, hidden):
    smem = pl.BlockSpec(memory_space=SMEM)
    hbm = pl.BlockSpec(memory_space=pltpu.HBM)
    return pl.pallas_call(
        densify_body,
        out_shape=(
            VMEM((width, hidden), BF16),
            VMEM((width, hidden), BF16),
            VMEM((hidden, width), BF16),
        ),
        in_specs=[smem] * 3 + [hbm] * 3,
        out_specs=(in_vmem(),) * 3,
        scratch_shapes=[pltpu.SemaphoreType.DMA((3,))],
        compiler_params=pltpu.CompilerParams(vmem_limit_bytes=2 * 2**20),
        name="densify",
    )(
        gate_index,
        up_index,
        down_index,
        *(pltpu.with_memory_space_constraint(x, pltpu.HBM) for x in (gate_blocks, up_blocks, down_blocks)),
    )


def activations(x, wg, wu, wd, hid, gp, up):
    width = wg.shape[0]
    hidden = wg.shape[1]
    chunk = 256 if hidden % 256 == 0 else 128

    def step(n, carry):
        cols = pl.ds(pl.multiple_of(n * chunk, chunk), chunk)
        g = dot_nn(x[:, :width], wg[:, cols])
        u = dot_nn(x[:, :width], wu[:, cols])
        h = dot_nt(x[:, width:], wd[cols, :])
        s = jax.nn.sigmoid(g)
        hid[:, cols] = (g * s * u).astype(BF16)
        gp[:, cols] = (h * u * s * (1.0 + g * (1.0 - s))).astype(BF16)
        up[:, cols] = (h * g * s).astype(BF16)
        return carry

    lax.fori_loop(0, hidden // chunk, step, 0)


def own_body(x, wg, wu, wd, hid, gp, up, part):
    activations(x, wg, wu, wd, hid, gp, up)
    width = wg.shape[0]
    chunk = 512

    def step(n, carry):
        cols = pl.ds(pl.multiple_of(n * chunk, chunk), chunk)
        later = pl.ds(pl.multiple_of(width + n * chunk, chunk), chunk)
        part[:, cols] = dot_nn(hid[...], wd[:, cols]).astype(BF16)
        part[:, later] = (dot_nt(gp[...], wg[cols, :]) + dot_nt(up[...], wu[cols, :])).astype(BF16)
        return carry

    lax.fori_loop(0, width // chunk, step, 0)


def own_pass(x, wg, wu, wd):
    rows = x.shape[0]
    width, hidden = wg.shape
    act = jax.ShapeDtypeStruct((rows, hidden), BF16)
    return pl.pallas_call(
        own_body,
        out_shape=(act, act, act, jax.ShapeDtypeStruct((rows, 2 * width), BF16)),
        in_specs=[in_vmem()] * 4,
        out_specs=(in_vmem(),) * 4,
        compiler_params=pltpu.CompilerParams(vmem_limit_bytes=8 * 2**20),
        cost_estimate=pl.CostEstimate(
            flops=12 * rows * width * hidden, bytes_accessed=2**20, transcendentals=0
        ),
        name="own_pass",
    )(x, *pinned(wg, wu, wd))


def rest_body(xa, xb, wg, wu, wd, hid, gp, up, x, sem):
    half = xa.shape[0]
    copies = [
        pltpu.make_async_copy(xa, x.at[pl.ds(0, half)], sem.at[0]),
        pltpu.make_async_copy(xb, x.at[pl.ds(half, half)], sem.at[1]),
    ]
    for copy in copies:
        copy.start()
    for copy in copies:
        copy.wait()
    activations(x, wg, wu, wd, hid, gp, up)


def rest_pass(xa, xb, wg, wu, wd):
    rows = 2 * xa.shape[0]
    width, hidden = wg.shape
    act = jax.ShapeDtypeStruct((rows, hidden), BF16)
    need = rows * (2 * width + 3 * hidden) * 2
    return pl.pallas_call(
        rest_body,
        out_shape=(act, act, act),
        in_specs=[pl.BlockSpec(memory_space=pl.ANY)] * 2 + [in_vmem()] * 3,
        out_specs=(in_vmem(),) * 3,
        scratch_shapes=[VMEM((rows, 2 * width), BF16), pltpu.SemaphoreType.DMA((2,))],
        compiler_params=pltpu.CompilerParams(vmem_limit_bytes=need + 4 * 2**20),
        cost_estimate=pl.CostEstimate(
            flops=6 * rows * width * hidden, bytes_accessed=2**20, transcendentals=0
        ),
        name="rest_pass",
    )(xa, xb, *pinned(wg, wu, wd))


def grads_body(
    factor, size, spots, own, xa, xb, hid0, hid1, gp0, gp1, up0, up1,
    gate_out, up_out, down_out, tok, tok_t, hid, hid_t, gp, up, cot, sem,
):
    i = pl.program_id(0)
    per_step = gate_out.shape[0]
    d_cols = tok_t.shape[0]
    ff_cols = hid_t.shape[0]
    width = d_cols * size
    first, half = own.shape[0], xa.shape[0]

    @pl.when(i == 0)
    def _():
        def parts(n, dst, sources):
            at, out = 0, []
            for src in sources:
                rows = src.shape[0]
                out.append(pltpu.make_async_copy(src, dst.at[pl.ds(at, rows)], sem.at[n]))
                at += rows
            return out

        def side(lo):
            return [x.at[:, pl.ds(lo, width)] for x in (own, xa, xb)]

        copies = [
            parts(0, tok, side(0)),
            parts(1, hid, (hid0, hid1)),
            parts(2, gp, (gp0, gp1)),
            parts(3, up, (up0, up1)),
            parts(4, cot, side(width)),
        ]
        for group in copies:
            for copy in group:
                copy.start()

        def turn(src, dst):
            def step(n, carry):
                cols = pl.ds(pl.multiple_of(n * size, size), size)
                dst[n] = src[:, cols].T
                return carry

            lax.fori_loop(0, dst.shape[0], step, 0)

        pltpu.make_async_copy(tok, tok, sem.at[0]).wait()
        turn(tok, tok_t)
        pltpu.make_async_copy(hid, hid, sem.at[1]).wait()
        turn(hid, hid_t)
        for n, ref in ((2, gp), (3, up), (4, cot)):
            pltpu.make_async_copy(ref, ref, sem.at[n]).wait()

    def one(which, left, right, out, cols, j):
        spot = spots[which, i * per_step + j]
        b = jnp.maximum(spot, 0)
        c = pl.multiple_of((b % cols) * size, size)
        value = dot_nn(left[b // cols], right[:, pl.ds(c, size)]) * factor
        out[j] = jnp.where(spot >= 0, value, 0.0)

    for j in range(per_step):
        one(0, tok_t, gp, gate_out, ff_cols, j)
        one(1, tok_t, up, up_out, ff_cols, j)
        one(2, hid_t, cot, down_out, d_cols, j)


def grads(spots, own, xa, xb, acts0, acts1, size, cap, factor):
    per_step = max(n for n in range(1, 18) if cap % n == 0 and (cap > n or cap < 18))
    per_step = min(per_step, 10) if cap % 10 == 0 else per_step
    width = own.shape[1] // 2
    hidden = acts0[0].shape[1]
    rows = own.shape[0] + 2 * xa.shape[0]
    out = jax.ShapeDtypeStruct((cap, size, size), F32)
    block = pl.BlockSpec((per_step, size, size), lambda i: (i, 0, 0))
    scratch = [
        VMEM((rows, width), BF16),
        VMEM((width // size, size, rows), BF16),
        VMEM((rows, hidden), BF16),
        VMEM((hidden // size, size, rows), BF16),
        VMEM((rows, hidden), BF16),
        VMEM((rows, hidden), BF16),
        VMEM((rows, width), BF16),
    ]
    need = rows * (3 * width + 4 * hidden) * 2 + per_step * 6 * size * size * 4
    return pl.pallas_call(
        functools.partial(grads_body, factor, size),
        out_shape=(out, out, out),
        grid=(cap // per_step,),
        in_specs=[pl.BlockSpec(memory_space=SMEM)] + [pl.BlockSpec(memory_space=pl.ANY)] * 9,
        out_specs=(block, block, block),
        scratch_shapes=scratch + [pltpu.SemaphoreType.DMA((5,))],
        compiler_params=pltpu.CompilerParams(vmem_limit_bytes=need + 2**20),
        cost_estimate=pl.CostEstimate(
            flops=6 * cap * size * size * rows, bytes_accessed=12 * cap * size * size, transcendentals=0
        ),
        name="grads",
    )(spots, own, xa, xb, acts0[0], acts1[0], acts0[1], acts1[1], acts0[2], acts1[2])


def local(
    tokens,
    out_grad,
    gate_blocks,
    up_blocks,
    down_blocks,
    gate_index,
    up_index,
    down_index,
    gate_slot,
    up_slot,
    down_slot,
):
    rows, width = tokens.shape
    size = gate_blocks.shape[1]
    kept_count = gate_blocks.shape[0]
    groups = lax.axis_size("dp")
    slices = lax.axis_size("tensor")
    hidden = FF // slices
    cap = (kept_count + groups - 1) // groups + kept_count // (4 * groups)
    factor = 1.0 / math.sqrt(rows * slices * groups)

    wg, wu, wd = densify(
        gate_index, up_index, down_index, gate_blocks, up_blocks, down_blocks, width, hidden
    )

    mine = lax.axis_index("dp") * cap + jnp.arange(cap, dtype=jnp.int32)
    slots = jnp.concatenate([gate_slot, up_slot, down_slot])
    index = jnp.concatenate([gate_index, up_index, down_index])
    hit = slots[:, None, :] == mine[None, :, None]
    spots = jnp.sum(jnp.where(hit, index[:, None, :] + 1, 0), axis=2) - 1

    both = jnp.concatenate([tokens, out_grad], axis=1)
    pairs = range(2, slices, 2)

    def over_chips(x):
        return jnp.concatenate([x] + [exchange(x, "tensor", d) for d in pairs], axis=0)

    own_half = over_chips(both)
    own = jnp.concatenate([own_half, exchange(own_half, "tensor", 1)], axis=0)
    others = jnp.concatenate([exchange(both, "dp", a) for a in range(1, groups)], axis=0)
    xa = over_chips(others)
    xb = exchange(xa, "tensor", 1)

    *acts0, part = own_pass(own, wg, wu, wd)
    acts1 = rest_pass(xa, xb, wg, wu, wd)

    half = own_half.shape[0]
    chip = part[:half].astype(F32) + exchange(part[half:], "tensor", 1).astype(F32)
    chip = chip.astype(BF16).reshape(slices // 2, rows, 2 * width)
    total = chip[0].astype(F32)
    for n, d in enumerate(pairs):
        total = total + exchange(chip[n + 1], "tensor", d).astype(F32)
    total = total.astype(BF16)

    gate_out, up_out, down_out = grads(spots, own, xa, xb, acts0, acts1, size, cap, factor)
    return (total[:, :width], total[:, width:], gate_out[None], up_out[None], down_out[None])


def solution(mesh):
    in_specs = (
        P(("dp", "tensor"), None),
        P(("dp", "tensor"), None),
        P("tensor", None, None),
        P("tensor", None, None),
        P("tensor", None, None),
        P("tensor", None),
        P("tensor", None),
        P("tensor", None),
        P("tensor", None),
        P("tensor", None),
        P("tensor", None),
    )
    out_specs = (
        P(("dp", "tensor"), None),
        P(("dp", "tensor"), None),
        P("tensor", "dp", None, None),
        P("tensor", "dp", None, None),
        P("tensor", "dp", None, None),
    )
    return jax.shard_map(local, mesh=mesh, in_specs=in_specs, out_specs=out_specs, check_vma=False)
```

```python
import functools
import math

import jax
import jax.numpy as jnp
from jax import lax
from jax.experimental import pallas as pl
from jax.experimental.pallas import tpu as pltpu
from jax.sharding import PartitionSpec as P

FF = 14336
BF16 = jnp.bfloat16
F32 = jnp.float32
VMEM = pltpu.VMEM
SMEM = pltpu.SMEM


SMEM_SPEC = pl.BlockSpec(memory_space=SMEM)
HBM_SPEC = pl.BlockSpec(memory_space=pltpu.HBM)
ANY_SPEC = pl.BlockSpec(memory_space=pl.ANY)
FREE = pl.CostEstimate(flops=0, bytes_accessed=0, transcendentals=0)
LIMIT = pltpu.CompilerParams(vmem_limit_bytes=4 * 2**20)


def in_vmem():
    return pl.BlockSpec(memory_space=VMEM)


def pinned(*arrays):
    return [pltpu.with_memory_space_constraint(x, VMEM) for x in arrays]


def in_hbm(x):
    return pltpu.with_memory_space_constraint(x, pltpu.HBM)


def dot_nn(a, b):
    return lax.dot_general(a, b, (((1,), (0,)), ((), ())), preferred_element_type=F32)


def dot_nt(a, b):
    return lax.dot_general(a, b, (((1,), (1,)), ((), ())), preferred_element_type=F32)


def exchange(x, axis, flip):
    count = lax.axis_size(axis)
    return lax.ppermute(x, axis, [(i, i ^ flip) for i in range(count)])


def assemble(pieces, out):
    chunk = 1024

    def step(n, carry):
        cols = pl.ds(pl.multiple_of(n * chunk, chunk), chunk)
        parts = [x[:, cols].astype(F32) for x in pieces]
        out[:, cols] = jnp.concatenate(parts, axis=0).astype(BF16)
        return carry

    lax.fori_loop(0, out.shape[1] // chunk, step, 0)


def pack(pieces, wait_for=()):
    rows = sum(x.shape[0] for x in pieces)
    width = pieces[0].shape[1]

    def body(*refs):
        assemble(refs[: len(pieces)], refs[-1])

    return pl.pallas_call(
        body,
        out_shape=jax.ShapeDtypeStruct((rows, width), BF16),
        in_specs=[in_vmem()] * len(pieces) + [ANY_SPEC] * len(wait_for),
        out_specs=in_vmem(),
        compiler_params=LIMIT,
        cost_estimate=FREE,
        name="pack",
    )(*pieces, *wait_for)


def side_by_side(left, right):
    rows, width = left.shape

    def body(left_ref, right_ref, out, sem):
        copies = [
            pltpu.make_async_copy(left_ref, out.at[:, pl.ds(0, width)], sem.at[0]),
            pltpu.make_async_copy(right_ref, out.at[:, pl.ds(width, width)], sem.at[1]),
        ]
        for copy in copies:
            copy.start()
        for copy in copies:
            copy.wait()

    return pl.pallas_call(
        body,
        out_shape=jax.ShapeDtypeStruct((rows, 2 * width), BF16),
        in_specs=[HBM_SPEC] * 2,
        out_specs=in_vmem(),
        scratch_shapes=[pltpu.SemaphoreType.DMA((2,))],
        compiler_params=LIMIT,
        name="side_by_side",
    )(in_hbm(left), in_hbm(right))


def add_and_cut(parts, sent, pieces):
    rows, width = sent[0].shape
    height = rows // pieces
    count = len(parts)

    def body(*refs):
        outs = refs[2 * count :]
        chunk = 1024
        for m in range(count):

            def step(n, carry):
                cols = pl.ds(pl.multiple_of(n * chunk, chunk), chunk)
                there = pl.ds(pl.multiple_of(m * width + n * chunk, chunk), chunk)
                total = refs[m][:, cols].astype(F32) + refs[count + m][:, cols].astype(F32)
                for i, out in enumerate(outs):
                    out[:, there] = total[i * height : (i + 1) * height].astype(BF16)
                return carry

            lax.fori_loop(0, width // chunk, step, 0)

    out = (jax.ShapeDtypeStruct((height, count * width), BF16),) * pieces
    return pl.pallas_call(
        body,
        out_shape=out,
        in_specs=[in_vmem()] * (2 * count),
        out_specs=(in_vmem(),) * pieces,
        compiler_params=LIMIT,
        cost_estimate=FREE,
        name="add_and_cut",
    )(*parts, *sent)


def scatter(index, blocks, dense, sem, other=None):
    kept, size = blocks.shape[0], blocks.shape[1]
    cols = dense.shape[1] // size
    unroll = 8 if kept % 8 == 0 else 1
    scale = 2**16 // cols + 1
    steps = kept // unroll
    rows = 0 if other is None else other.shape[0] // steps // 16 * 16

    def step(i, carry):
        for u in range(unroll):
            k = i * unroll + u
            b = index[0, k]
            r = lax.shift_right_logical(b * scale, 16)
            c = b - r * cols
            r, c = pl.multiple_of(r * size, size), pl.multiple_of(c * size, size)
            pltpu.make_async_copy(
                blocks.at[k], dense.at[pl.ds(r, size), pl.ds(c, size)], sem
            ).start()
        if rows:
            part = pl.ds(pl.multiple_of(i * rows, rows), rows)
            other[part] = jnp.zeros((rows, other.shape[1]), BF16)
        return carry

    lax.fori_loop(0, steps, step, 0)
    if other is not None and other.shape[0] > steps * rows:
        left = other.shape[0] - steps * rows
        other[pl.ds(steps * rows, left)] = jnp.zeros((left, other.shape[1]), BF16)


def dense_gate_body(index, blocks, *refs):
    wg, sem = refs[-2:]
    wg[...] = jnp.zeros_like(wg)
    scatter(index, blocks, wg, sem)
    pltpu.make_async_copy(blocks, blocks, sem).wait()


def dense_both_body(ui, di, ub, db, wu, wd, stage, sem):
    stage[...] = jnp.zeros_like(stage)
    scatter(di, db, stage, sem.at[0], wu)
    scatter(ui, ub, wu, sem.at[2])
    pltpu.make_async_copy(db, db, sem.at[0]).wait()
    pltpu.make_async_copy(stage, wd, sem.at[1]).start()
    pltpu.make_async_copy(ub, ub, sem.at[2]).wait()
    pltpu.make_async_copy(stage, wd, sem.at[1]).wait()


def dense_gate(index, blocks, width, hidden, wait_for):
    return pl.pallas_call(
        dense_gate_body,
        out_shape=VMEM((width, hidden), BF16),
        in_specs=[SMEM_SPEC, HBM_SPEC] + [ANY_SPEC] * len(wait_for),
        out_specs=in_vmem(),
        scratch_shapes=[pltpu.SemaphoreType.DMA],
        compiler_params=pltpu.CompilerParams(vmem_limit_bytes=2**20),
        cost_estimate=FREE,
        name="dense_gate",
    )(index, in_hbm(blocks), *wait_for)


def dense_both(up_index, down_index, up_blocks, down_blocks, width, hidden):
    return pl.pallas_call(
        dense_both_body,
        out_shape=(VMEM((width, hidden), BF16), pltpu.HBM((hidden, width), BF16)),
        in_specs=[SMEM_SPEC] * 2 + [HBM_SPEC] * 2,
        out_specs=(in_vmem(), HBM_SPEC),
        scratch_shapes=[VMEM((hidden, width), BF16), pltpu.SemaphoreType.DMA((3,))],
        compiler_params=pltpu.CompilerParams(vmem_limit_bytes=2 * hidden * width + 2**20),
        cost_estimate=FREE,
        name="dense_both",
    )(up_index, down_index, in_hbm(up_blocks), in_hbm(down_blocks))


def chunk_of(hidden):
    return 256 if hidden % 256 == 0 else 128


def activations(tok, cot, wg, wu, wd):
    g = dot_nn(tok[...], wg)
    u = dot_nn(tok[...], wu)
    h = dot_nt(cot[...], wd)
    s = jax.nn.sigmoid(g)
    hid = (g * s * u).astype(BF16)
    gp = (h * u * s * (1.0 + g * (1.0 - s))).astype(BF16)
    up = (h * g * s).astype(BF16)
    return hid, gp, up


def acts_body(count, *refs):
    pieces, (wg, wu, wd), (hid, gp, up, x) = refs[:count], refs[count : count + 3], refs[-4:]
    n = pl.program_id(0)
    width, chunk = wg.shape[0], wd.shape[0]

    @pl.when(n == 0)
    def _():
        assemble(pieces, x)

    cols = pl.ds(pl.multiple_of(n * chunk, chunk), chunk)
    tok, cot = x.at[:, pl.ds(0, width)], x.at[:, pl.ds(width, width)]
    hid[...], gp[...], up[...] = activations(tok, cot, wg[:, cols], wu[:, cols], wd[...])


def acts_pass(pieces, wg, wu, wd, name, wait_for=()):
    rows = sum(x.shape[0] for x in pieces)
    width, hidden = wg.shape
    chunk = chunk_of(hidden)
    act = jax.ShapeDtypeStruct((rows, hidden), BF16)
    piece = pl.BlockSpec((rows, chunk), lambda n: (0, n))
    need = 84 * rows * chunk + 4 * chunk * width
    return pl.pallas_call(
        functools.partial(acts_body, len(pieces)),
        out_shape=(act, act, act, VMEM((rows, 2 * width), BF16)),
        grid=(hidden // chunk,),
        in_specs=[in_vmem()] * (len(pieces) + 2)
        + [pl.BlockSpec((chunk, width), lambda n: (n, 0))]
        + [ANY_SPEC] * len(wait_for),
        out_specs=(piece, piece, piece, in_vmem()),
        compiler_params=pltpu.CompilerParams(vmem_limit_bytes=max(need, 8 * 2**20)),
        cost_estimate=pl.CostEstimate(
            flops=6 * rows * width * hidden, bytes_accessed=2 * width * hidden, transcendentals=0
        ),
        name=name,
    )(*pieces, *pinned(wg, wu), in_hbm(wd), *wait_for)


def own_out_body(hid, gp, up, wg, wu, wd, part, back):
    n = pl.program_id(0)
    chunk = wd.shape[1]
    width = wg.shape[0]
    half = part.shape[0]
    out = pl.ds(pl.multiple_of(n * chunk, chunk), chunk)
    later = pl.ds(pl.multiple_of(width + n * chunk, chunk), chunk)
    left = dot_nn(hid[...], wd[...]).astype(BF16)
    right = (dot_nt(gp[...], wg[out, :]) + dot_nt(up[...], wu[out, :])).astype(BF16)
    part[:, out] = left[:half]
    back[:, out] = left[half:]
    part[:, later] = right[:half]
    back[:, later] = right[half:]


def own_out(hid, gp, up, wg, wu, wd):
    rows = hid.shape[0]
    width, hidden = wg.shape
    chunk = 512
    return pl.pallas_call(
        own_out_body,
        out_shape=(jax.ShapeDtypeStruct((rows // 2, 2 * width), BF16),) * 2,
        grid=(width // chunk,),
        in_specs=[in_vmem()] * 5 + [pl.BlockSpec((hidden, chunk), lambda n: (0, n))],
        out_specs=(in_vmem(), in_vmem()),
        compiler_params=pltpu.CompilerParams(
            vmem_limit_bytes=max(4 * chunk * hidden + 16 * rows * chunk + 2**21, 7 * 2**20)
        ),
        cost_estimate=pl.CostEstimate(
            flops=6 * rows * width * hidden, bytes_accessed=2 * width * hidden, transcendentals=0
        ),
        name="own_out",
    )(hid, gp, up, *pinned(wg, wu), in_hbm(wd))


def grads_body(
    factor, size, spots, own, rest, hid0, hid1, gp0, gp1, up0, up1,
    gate_out, up_out, down_out, tok_t, hid_t,
):
    i = pl.program_id(0)
    steps = pl.num_programs(0) // 2
    per_step = gate_out.shape[0]
    d_cols = tok_t.shape[0]
    ff_cols = hid_t.shape[0]
    width = d_cols * size

    def column(first, second, start):
        cols = pl.ds(pl.multiple_of(start, size), size)
        return jnp.concatenate([first[:, cols], second[:, cols]], axis=0)

    def one(which, left, first, second, base, out, cols, at, j):
        spot = spots[which, at * per_step + j]
        b = jnp.maximum(spot, 0)
        r = lax.shift_right_logical(b * (2**16 // cols + 1), 16)
        c = b - r * cols
        value = dot_nn(left[r], column(first, second, base + c * size)) * factor
        out[j] = jnp.where(spot >= 0, value, 0.0)

    @pl.when(i == 0)
    def _():
        def step(n, carry):
            hid_t[n] = column(hid0, hid1, n * size).T
            return carry

        lax.fori_loop(0, ff_cols, step, 0)

    @pl.when(i < steps)
    def _():
        turns = -(-d_cols // (spots.shape[1] // per_step))
        for j in range(max(per_step, turns)):
            if j < turns:
                n = jnp.minimum(i * turns + j, d_cols - 1)
                tok_t[n] = column(own, rest, n * size).T
            if j < per_step:
                one(2, hid_t, own, rest, width, down_out, d_cols, i, j)

    @pl.when(i >= steps)
    def _():
        for j in range(per_step):
            one(0, tok_t, gp0, gp1, 0, gate_out, ff_cols, i - steps, j)
            one(1, tok_t, up0, up1, 0, up_out, ff_cols, i - steps, j)


def grads(spots, own, rest, acts0, acts1, size, cap, factor):
    per_step = max(n for n in range(1, 18) if cap % n == 0)
    per_step = 10 if cap % 10 == 0 else per_step
    steps = cap // per_step
    width = own.shape[1] // 2
    hidden = acts0[0].shape[1]
    rows = own.shape[0] + rest.shape[0]
    out = jax.ShapeDtypeStruct((cap, size, size), F32)
    early = pl.BlockSpec((per_step, size, size), lambda i: (jnp.minimum(i, steps - 1), 0, 0))
    late = pl.BlockSpec((per_step, size, size), lambda i: (jnp.maximum(i - steps, 0), 0, 0))
    need = rows * (6 * width + 8 * hidden) + per_step * 6 * size * size * 4
    return pl.pallas_call(
        functools.partial(grads_body, factor, size),
        out_shape=(out, out, out),
        grid=(2 * steps,),
        in_specs=[SMEM_SPEC] + [in_vmem()] * 8,
        out_specs=(late, late, early),
        scratch_shapes=[
            VMEM((width // size, size, rows), BF16),
            VMEM((hidden // size, size, rows), BF16),
        ],
        compiler_params=pltpu.CompilerParams(vmem_limit_bytes=need + 2**21),
        cost_estimate=pl.CostEstimate(
            flops=6 * cap * size * size * rows, bytes_accessed=12 * cap * size * size, transcendentals=0
        ),
        name="grads",
    )(spots, own, rest, acts0[0], acts1[0], acts0[1], acts1[1], acts0[2], acts1[2])


def local(
    tokens,
    out_grad,
    gate_blocks,
    up_blocks,
    down_blocks,
    gate_index,
    up_index,
    down_index,
    gate_slot,
    up_slot,
    down_slot,
):
    rows, width = tokens.shape
    size = gate_blocks.shape[1]
    kept_count = gate_blocks.shape[0]
    groups = lax.axis_size("dp")
    slices = lax.axis_size("tensor")
    hidden = FF // slices
    cap = (kept_count + groups - 1) // groups + kept_count // (4 * groups)
    factor = 1.0 / math.sqrt(rows * slices * groups)

    mine = lax.axis_index("dp") * cap + jnp.arange(cap, dtype=jnp.int32)
    slots = jnp.concatenate([gate_slot, up_slot, down_slot])
    index = jnp.concatenate([gate_index, up_index, down_index])
    hit = slots[:, None, :] == mine[None, :, None]
    spots = jnp.sum(jnp.where(hit, index[:, None, :] + 1, 0), axis=2) - 1

    both = side_by_side(tokens, out_grad)
    chips = range(2, slices, 2)

    def sibling(x):
        return exchange(x, "tensor", 1)

    far = [exchange(both, "dp", a) for a in range(1, groups)]
    near = [exchange(both, "tensor", d) for d in chips]
    wu, wd = dense_both(up_index, down_index, up_blocks, down_blocks, width, hidden)
    own_half = pack([both, *near], [wu])
    others = pack(far, [wu])
    wg = dense_gate(gate_index, gate_blocks, width, hidden, [own_half, others, spots])
    own_pieces = [own_half, sibling(own_half)]
    other_half = [others, *(exchange(others, "tensor", d) for d in chips)]

    *acts0, own = acts_pass(own_pieces, wg, wu, wd, "own_acts")
    part, back = own_out(*acts0, wg, wu, wd)
    chip = add_and_cut([part], [sibling(back)], slices // 2)
    acts1_in = [*other_half, *(sibling(x) for x in other_half)]
    *acts1, rest = acts_pass(acts1_in, wg, wu, wd, "rest_acts", [chip[0]])

    total = chip[0].astype(F32)
    for piece, d in zip(chip[1:], chips):
        total = total + exchange(piece, "tensor", d).astype(F32)
    total = total.astype(BF16)

    gate_out, up_out, down_out = grads(spots, own, rest, acts0, acts1, size, cap, factor)
    return (total[:, :width], total[:, width:], gate_out[None], up_out[None], down_out[None])


def solution(mesh):
    in_specs = (
        P(("dp", "tensor"), None),
        P(("dp", "tensor"), None),
        P("tensor", None, None),
        P("tensor", None, None),
        P("tensor", None, None),
        P("tensor", None),
        P("tensor", None),
        P("tensor", None),
        P("tensor", None),
        P("tensor", None),
        P("tensor", None),
    )
    out_specs = (
        P(("dp", "tensor"), None),
        P(("dp", "tensor"), None),
        P("tensor", "dp", None, None),
        P("tensor", "dp", None, None),
        P("tensor", "dp", None, None),
    )
    return jax.shard_map(local, mesh=mesh, in_specs=in_specs, out_specs=out_specs, check_vma=False)
```

```python
import functools
import math

import jax
import jax.numpy as jnp
from jax import lax
from jax.experimental import pallas as pl
from jax.experimental.pallas import tpu as pltpu
from jax.sharding import PartitionSpec as P

FF = 14336
BF16 = jnp.bfloat16
F32 = jnp.float32
VMEM = pltpu.VMEM
SMEM = pltpu.SMEM


SMEM_SPEC = pl.BlockSpec(memory_space=SMEM)
HBM_SPEC = pl.BlockSpec(memory_space=pltpu.HBM)
ANY_SPEC = pl.BlockSpec(memory_space=pl.ANY)
FREE = pl.CostEstimate(flops=0, bytes_accessed=0, transcendentals=0)
LIMIT = pltpu.CompilerParams(vmem_limit_bytes=4 * 2**20)
DENSE_LIMIT = 17 * 2**20
NEXT_LIMIT = 17 * 2**20


def in_vmem():
    return pl.BlockSpec(memory_space=VMEM)


def pinned(*arrays):
    return [pltpu.with_memory_space_constraint(x, VMEM) for x in arrays]


def in_hbm(x):
    return pltpu.with_memory_space_constraint(x, pltpu.HBM)


def dot_nn(a, b):
    return lax.dot_general(a, b, (((1,), (0,)), ((), ())), preferred_element_type=F32)


def dot_nt(a, b):
    return lax.dot_general(a, b, (((1,), (1,)), ((), ())), preferred_element_type=F32)


def exchange(x, axis, flip):
    count = lax.axis_size(axis)
    return lax.ppermute(x, axis, [(i, i ^ flip) for i in range(count)])


def assemble(pieces, out):
    chunk = 1024

    def step(n, carry):
        cols = pl.ds(pl.multiple_of(n * chunk, chunk), chunk)
        parts = [x[:, cols].astype(F32) for x in pieces]
        out[:, cols] = jnp.concatenate(parts, axis=0).astype(BF16)
        return carry

    lax.fori_loop(0, out.shape[1] // chunk, step, 0)


def pack(pieces, wait_for=()):
    rows = sum(x.shape[0] for x in pieces)
    width = pieces[0].shape[1]

    def body(*refs):
        assemble(refs[: len(pieces)], refs[-1])

    return pl.pallas_call(
        body,
        out_shape=jax.ShapeDtypeStruct((rows, width), BF16),
        in_specs=[in_vmem()] * len(pieces) + [ANY_SPEC] * len(wait_for),
        out_specs=in_vmem(),
        compiler_params=LIMIT,
        cost_estimate=FREE,
        name="pack",
    )(*pieces, *wait_for)


def side_by_side(left, right):
    rows, width = left.shape

    def body(left_ref, right_ref, out, sem):
        copies = [
            pltpu.make_async_copy(left_ref, out.at[:, pl.ds(0, width)], sem.at[0]),
            pltpu.make_async_copy(right_ref, out.at[:, pl.ds(width, width)], sem.at[1]),
        ]
        for copy in copies:
            copy.start()
        for copy in copies:
            copy.wait()

    return pl.pallas_call(
        body,
        out_shape=jax.ShapeDtypeStruct((rows, 2 * width), BF16),
        in_specs=[HBM_SPEC] * 2,
        out_specs=in_vmem(),
        scratch_shapes=[pltpu.SemaphoreType.DMA((2,))],
        compiler_params=LIMIT,
        name="side_by_side",
    )(in_hbm(left), in_hbm(right))


def add_and_cut(parts, sent, pieces):
    rows, width = sent[0].shape
    height = rows // pieces
    count = len(parts)

    def body(*refs):
        outs = refs[2 * count :]
        chunk = 1024
        for m in range(count):

            def step(n, carry):
                cols = pl.ds(pl.multiple_of(n * chunk, chunk), chunk)
                there = pl.ds(pl.multiple_of(m * width + n * chunk, chunk), chunk)
                total = refs[m][:, cols].astype(F32) + refs[count + m][:, cols].astype(F32)
                for i, out in enumerate(outs):
                    out[:, there] = total[i * height : (i + 1) * height].astype(BF16)
                return carry

            lax.fori_loop(0, width // chunk, step, 0)

    out = (jax.ShapeDtypeStruct((height, count * width), BF16),) * pieces
    return pl.pallas_call(
        body,
        out_shape=out,
        in_specs=[in_vmem()] * (2 * count),
        out_specs=(in_vmem(),) * pieces,
        compiler_params=LIMIT,
        cost_estimate=FREE,
        name="add_and_cut",
    )(*parts, *sent)


def scatter(index, blocks, dense, sem, first, count):
    size = blocks.shape[1]
    cols = dense.shape[1] // size
    scale = 2**16 // cols + 1
    for u in range(count):
        k = first + u
        b = index[0, k]
        r = lax.shift_right_logical(b * scale, 16)
        c = b - r * cols
        r, c = pl.multiple_of(r * size, size), pl.multiple_of(c * size, size)
        pltpu.make_async_copy(
            blocks.at[k], dense.at[pl.ds(r, size), pl.ds(c, size)], sem
        ).start()


def dense_body(again, index_hbm, blocks, *refs):
    if again:
        source, dense, copied, index, sem = refs[0], *refs[-4:]
        copy = pltpu.make_async_copy(source, copied, sem.at[2])
        copy.start()
    else:
        dense, index, sem = refs[-3:]
    fetch = pltpu.make_async_copy(index_hbm, index, sem.at[1])
    fetch.start()
    dense[...] = jnp.zeros_like(dense)
    fetch.wait()
    kept = blocks.shape[0]
    unroll = 8 if kept % 8 == 0 else 1

    def step(i, carry):
        scatter(index, blocks, dense, sem.at[0], i * unroll, unroll)
        return carry

    lax.fori_loop(0, kept // unroll, step, 0)
    if again:
        copy.wait()
    pltpu.make_async_copy(blocks, blocks, sem.at[0]).wait()


def dense(index, blocks, source, width, hidden, limit, wait_for=()):
    again = [] if source is None else [source]
    outs = [VMEM((width, hidden), BF16)] + [VMEM(x.shape, x.dtype) for x in again]
    return pl.pallas_call(
        functools.partial(dense_body, bool(again)),
        out_shape=outs,
        in_specs=[HBM_SPEC] * 2 + [ANY_SPEC] * (len(again) + len(wait_for)),
        out_specs=[in_vmem()] * len(outs),
        scratch_shapes=[pltpu.SMEM(index.shape, jnp.int32), pltpu.SemaphoreType.DMA((3,))],
        compiler_params=pltpu.CompilerParams(vmem_limit_bytes=limit),
        cost_estimate=FREE,
        name="dense",
    )(in_hbm(index), in_hbm(blocks), *again, *wait_for)


def chunk_of(hidden):
    return 256 if hidden % 256 == 0 else 128


def activations(tok, cot, wg, wu, wd):
    g = dot_nn(tok[...], wg)
    u = dot_nn(tok[...], wu)
    h = dot_nt(cot[...], wd)
    s = jax.nn.sigmoid(g)
    hid = (g * s * u).astype(BF16)
    gp = (h * u * s * (1.0 + g * (1.0 - s))).astype(BF16)
    up = (h * g * s).astype(BF16)
    return hid, gp, up


def acts_body(count, *refs):
    pieces, (wg, wu, wd), (hid, gp, up, x) = refs[:count], refs[count : count + 3], refs[-4:]
    n = pl.program_id(0)
    width, chunk = wg.shape[0], wd.shape[0]

    @pl.when(n == 0)
    def _():
        assemble(pieces, x)

    cols = pl.ds(pl.multiple_of(n * chunk, chunk), chunk)
    tok, cot = x.at[:, pl.ds(0, width)], x.at[:, pl.ds(width, width)]
    hid[...], gp[...], up[...] = activations(tok, cot, wg[:, cols], wu[:, cols], wd[...])


def acts_pass(pieces, wg, wu, wd, name, wait_for=()):
    rows = sum(x.shape[0] for x in pieces)
    width, hidden = wg.shape
    chunk = chunk_of(hidden)
    act = jax.ShapeDtypeStruct((rows, hidden), BF16)
    piece = pl.BlockSpec((rows, chunk), lambda n: (0, n))
    need = 84 * rows * chunk + 4 * chunk * width
    return pl.pallas_call(
        functools.partial(acts_body, len(pieces)),
        out_shape=(act, act, act, VMEM((rows, 2 * width), BF16)),
        grid=(hidden // chunk,),
        in_specs=[in_vmem()] * (len(pieces) + 2)
        + [pl.BlockSpec((chunk, width), lambda n: (n, 0))]
        + [ANY_SPEC] * len(wait_for),
        out_specs=(piece, piece, piece, in_vmem()),
        compiler_params=pltpu.CompilerParams(vmem_limit_bytes=max(need, 8 * 2**20)),
        cost_estimate=pl.CostEstimate(
            flops=6 * rows * width * hidden, bytes_accessed=2 * width * hidden, transcendentals=0
        ),
        name=name,
    )(*pieces, *pinned(wg, wu), in_hbm(wd), *wait_for)


def own_body(count, index_hbm, *refs):
    pieces, (wg, wu, blocks), refs = refs[:count], refs[count : count + 3], refs[count + 3 :]
    hid, gp, up, x, part, back, wd_out, wd, g_all, u_all, index, sem = refs
    width, hidden = wg.shape
    steps, _, chunk = g_all.shape
    kept = blocks.shape[0]
    each = kept // steps
    fetch = pltpu.make_async_copy(index_hbm, index, sem.at[1])
    fetch.start()
    assemble(pieces, x)

    def place(n):
        return pl.ds(pl.multiple_of(n * chunk, chunk), chunk)

    def gate(n, carry):
        g_all[n] = dot_nn(x[:, :width], wg[:, place(n)])
        wd[place(n)] = jnp.zeros((chunk, width), BF16)
        return carry

    lax.fori_loop(0, steps, gate, 0)
    fetch.wait()

    def up_proj(n, carry):
        scatter(index, blocks, wd, sem.at[0], n * each, each)
        u_all[n] = dot_nn(x[:, :width], wu[:, place(n)])
        return carry

    lax.fori_loop(0, steps, up_proj, 0)
    scatter(index, blocks, wd, sem.at[0], steps * each, kept - steps * each)
    pltpu.make_async_copy(blocks, blocks, sem.at[0]).wait()
    store = pltpu.make_async_copy(wd, wd_out, sem.at[2])
    store.start()

    def grad(n, carry):
        cols = place(n)
        g, u = g_all[n], u_all[n]
        h = dot_nt(x[:, width:], wd[cols])
        s = jax.nn.sigmoid(g)
        hid[:, cols] = (g * s * u).astype(BF16)
        gp[:, cols] = (h * u * s * (1.0 + g * (1.0 - s))).astype(BF16)
        up[:, cols] = (h * g * s).astype(BF16)
        return carry

    lax.fori_loop(0, steps, grad, 0)
    half = part.shape[0]
    wide = 512

    def sums(n, carry):
        out = pl.ds(pl.multiple_of(n * wide, wide), wide)
        later = pl.ds(pl.multiple_of(width + n * wide, wide), wide)
        left = dot_nn(hid[...], wd[:, out]).astype(BF16)
        right = (dot_nt(gp[...], wg[out, :]) + dot_nt(up[...], wu[out, :])).astype(BF16)
        part[:, out] = left[:half]
        back[:, out] = left[half:]
        part[:, later] = right[:half]
        back[:, later] = right[half:]
        return carry

    lax.fori_loop(0, width // wide, sums, 0)
    store.wait()


def own_pass(pieces, wg, wu, index, blocks, limit):
    rows = sum(x.shape[0] for x in pieces)
    width, hidden = wg.shape
    chunk = chunk_of(hidden)
    act = VMEM((rows, hidden), BF16)
    half = VMEM((rows // 2, 2 * width), BF16)
    kept = VMEM((hidden // chunk, rows, chunk), F32)
    return pl.pallas_call(
        functools.partial(own_body, len(pieces)),
        out_shape=(
            act, act, act, VMEM((rows, 2 * width), BF16), half, half,
            pltpu.HBM((hidden, width), BF16),
        ),
        in_specs=[HBM_SPEC] + [in_vmem()] * (len(pieces) + 2) + [HBM_SPEC],
        out_specs=(in_vmem(),) * 6 + (HBM_SPEC,),
        scratch_shapes=[
            VMEM((hidden, width), BF16),
            kept,
            kept,
            pltpu.SMEM(index.shape, jnp.int32),
            pltpu.SemaphoreType.DMA((3,)),
        ],
        compiler_params=pltpu.CompilerParams(vmem_limit_bytes=limit),
        cost_estimate=pl.CostEstimate(
            flops=12 * rows * width * hidden, bytes_accessed=2 * width * hidden, transcendentals=0
        ),
        name="own_pass",
    )(in_hbm(index), *pieces, *pinned(wg, wu), in_hbm(blocks))


def grads_body(
    factor, size, spots, own, rest, hid0, hid1, gp0, gp1, up0, up1,
    gate_out, up_out, down_out, tok_t, hid_t,
):
    i = pl.program_id(0)
    steps = pl.num_programs(0) // 2
    per_step = gate_out.shape[0]
    d_cols = tok_t.shape[0]
    ff_cols = hid_t.shape[0]
    width = d_cols * size

    def column(first, second, start):
        cols = pl.ds(pl.multiple_of(start, size), size)
        return jnp.concatenate([first[:, cols], second[:, cols]], axis=0)

    def one(which, left, first, second, base, out, cols, at, j):
        spot = spots[which, at * per_step + j]
        b = jnp.maximum(spot, 0)
        r = lax.shift_right_logical(b * (2**16 // cols + 1), 16)
        c = b - r * cols
        value = dot_nn(left[r], column(first, second, base + c * size)) * factor
        out[j] = jnp.where(spot >= 0, value, 0.0)

    @pl.when(i == 0)
    def _():
        def step(n, carry):
            hid_t[n] = column(hid0, hid1, n * size).T
            return carry

        lax.fori_loop(0, ff_cols, step, 0)

    @pl.when(i < steps)
    def _():
        turns = -(-d_cols // (spots.shape[1] // per_step))
        for j in range(max(per_step, turns)):
            if j < turns:
                n = jnp.minimum(i * turns + j, d_cols - 1)
                tok_t[n] = column(own, rest, n * size).T
            if j < per_step:
                one(2, hid_t, own, rest, width, down_out, d_cols, i, j)

    @pl.when(i >= steps)
    def _():
        for j in range(per_step):
            one(0, tok_t, gp0, gp1, 0, gate_out, ff_cols, i - steps, j)
            one(1, tok_t, up0, up1, 0, up_out, ff_cols, i - steps, j)


def grads(spots, own, rest, acts0, acts1, size, cap, factor):
    per_step = max(n for n in range(1, 18) if cap % n == 0)
    per_step = 10 if cap % 10 == 0 else per_step
    steps = cap // per_step
    width = own.shape[1] // 2
    hidden = acts0[0].shape[1]
    rows = own.shape[0] + rest.shape[0]
    out = jax.ShapeDtypeStruct((cap, size, size), F32)
    early = pl.BlockSpec((per_step, size, size), lambda i: (jnp.minimum(i, steps - 1), 0, 0))
    late = pl.BlockSpec((per_step, size, size), lambda i: (jnp.maximum(i - steps, 0), 0, 0))
    need = rows * (6 * width + 8 * hidden) + per_step * 6 * size * size * 4
    return pl.pallas_call(
        functools.partial(grads_body, factor, size),
        out_shape=(out, out, out),
        grid=(2 * steps,),
        in_specs=[SMEM_SPEC] + [in_vmem()] * 8,
        out_specs=(late, late, early),
        scratch_shapes=[
            VMEM((width // size, size, rows), BF16),
            VMEM((hidden // size, size, rows), BF16),
        ],
        compiler_params=pltpu.CompilerParams(vmem_limit_bytes=need + 2**21),
        cost_estimate=pl.CostEstimate(
            flops=6 * cap * size * size * rows, bytes_accessed=12 * cap * size * size, transcendentals=0
        ),
        name="grads",
    )(spots, own, rest, acts0[0], acts1[0], acts0[1], acts1[1], acts0[2], acts1[2])


def local(
    tokens,
    out_grad,
    gate_blocks,
    up_blocks,
    down_blocks,
    gate_index,
    up_index,
    down_index,
    gate_slot,
    up_slot,
    down_slot,
):
    rows, width = tokens.shape
    size = gate_blocks.shape[1]
    kept_count = gate_blocks.shape[0]
    groups = lax.axis_size("dp")
    slices = lax.axis_size("tensor")
    hidden = FF // slices
    cap = (kept_count + groups - 1) // groups + kept_count // (4 * groups)
    factor = 1.0 / math.sqrt(rows * slices * groups)

    mine = lax.axis_index("dp") * cap + jnp.arange(cap, dtype=jnp.int32)
    slots = jnp.concatenate([gate_slot, up_slot, down_slot])
    index = jnp.concatenate([gate_index, up_index, down_index])
    hit = slots[:, None, :] == mine[None, :, None]
    spots = jnp.sum(jnp.where(hit, index[:, None, :] + 1, 0), axis=2) - 1

    both = side_by_side(tokens, out_grad)
    chips = range(2, slices, 2)

    def sibling(x):
        return exchange(x, "tensor", 1)

    far = [exchange(both, "dp", a) for a in range(1, groups)]
    near = [exchange(both, "tensor", d) for d in chips[:-1]]
    stage = 2 * width * hidden
    wu, later = dense(up_index, up_blocks, both, width, hidden, DENSE_LIMIT)
    near.append(exchange(later, "tensor", chips[-1]))
    others = pack(far, [wu])
    (wg,) = dense(gate_index, gate_blocks, None, width, hidden, NEXT_LIMIT, [spots, others])
    own_half = pack([both, *near], [wg])
    own_pieces = [own_half, sibling(own_half)]
    other_half = [others, *(exchange(others, "tensor", d) for d in chips)]

    *acts0, own, part, back, wd = own_pass(
        own_pieces, wg, wu, down_index, down_blocks, stage + 3 * 2**20
    )
    chip = add_and_cut([part], [sibling(back)], slices // 2)
    acts1_in = [*other_half, *(sibling(x) for x in other_half)]
    *acts1, rest = acts_pass(acts1_in, wg, wu, wd, "rest_acts", [chip[0]])

    total = chip[0].astype(F32)
    for piece, d in zip(chip[1:], chips):
        total = total + exchange(piece, "tensor", d).astype(F32)
    total = total.astype(BF16)

    gate_out, up_out, down_out = grads(spots, own, rest, acts0, acts1, size, cap, factor)
    return (total[:, :width], total[:, width:], gate_out[None], up_out[None], down_out[None])


def solution(mesh):
    in_specs = (
        P(("dp", "tensor"), None),
        P(("dp", "tensor"), None),
        P("tensor", None, None),
        P("tensor", None, None),
        P("tensor", None, None),
        P("tensor", None),
        P("tensor", None),
        P("tensor", None),
        P("tensor", None),
        P("tensor", None),
        P("tensor", None),
    )
    out_specs = (
        P(("dp", "tensor"), None),
        P(("dp", "tensor"), None),
        P("tensor", "dp", None, None),
        P("tensor", "dp", None, None),
        P("tensor", "dp", None, None),
    )
    return jax.shard_map(local, mesh=mesh, in_specs=in_specs, out_specs=out_specs, check_vma=False)
```

```python
import functools
import math

import jax
import jax.numpy as jnp
from jax import lax
from jax.experimental import pallas as pl
from jax.experimental.pallas import tpu as pltpu
from jax.sharding import PartitionSpec as P

FF = 14336
BF16 = jnp.bfloat16
F32 = jnp.float32
VMEM = pltpu.VMEM
SMEM = pltpu.SMEM


SMEM_SPEC = pl.BlockSpec(memory_space=SMEM)
HBM_SPEC = pl.BlockSpec(memory_space=pltpu.HBM)
ANY_SPEC = pl.BlockSpec(memory_space=pl.ANY)
FREE = pl.CostEstimate(flops=0, bytes_accessed=0, transcendentals=0)
LIMIT = pltpu.CompilerParams(vmem_limit_bytes=4 * 2**20)
DENSE_LIMIT = 17 * 2**20
NEXT_LIMIT = 17 * 2**20


def in_vmem():
    return pl.BlockSpec(memory_space=VMEM)


def pinned(*arrays):
    return [pltpu.with_memory_space_constraint(x, VMEM) for x in arrays]


def in_hbm(x):
    return pltpu.with_memory_space_constraint(x, pltpu.HBM)


def dot_nn(a, b):
    return lax.dot_general(a, b, (((1,), (0,)), ((), ())), preferred_element_type=F32)


def dot_nt(a, b):
    return lax.dot_general(a, b, (((1,), (1,)), ((), ())), preferred_element_type=F32)


def exchange(x, axis, flip):
    count = lax.axis_size(axis)
    return lax.ppermute(x, axis, [(i, i ^ flip) for i in range(count)])


def assemble(pieces, out):
    chunk = 1024

    def step(n, carry):
        cols = pl.ds(pl.multiple_of(n * chunk, chunk), chunk)
        parts = [x[:, cols].astype(F32) for x in pieces]
        out[:, cols] = jnp.concatenate(parts, axis=0).astype(BF16)
        return carry

    lax.fori_loop(0, out.shape[1] // chunk, step, 0)


def pack(pieces, wait_for=()):
    rows = sum(x.shape[0] for x in pieces)
    width = pieces[0].shape[1]

    def body(*refs):
        assemble(refs[: len(pieces)], refs[-1])

    return pl.pallas_call(
        body,
        out_shape=jax.ShapeDtypeStruct((rows, width), BF16),
        in_specs=[in_vmem()] * len(pieces) + [ANY_SPEC] * len(wait_for),
        out_specs=in_vmem(),
        compiler_params=LIMIT,
        cost_estimate=FREE,
        name="pack",
    )(*pieces, *wait_for)


def side_by_side(left, right):
    rows, width = left.shape

    def body(left_ref, right_ref, out, sem):
        copies = [
            pltpu.make_async_copy(left_ref, out.at[:, pl.ds(0, width)], sem.at[0]),
            pltpu.make_async_copy(right_ref, out.at[:, pl.ds(width, width)], sem.at[1]),
        ]
        for copy in copies:
            copy.start()
        for copy in copies:
            copy.wait()

    return pl.pallas_call(
        body,
        out_shape=jax.ShapeDtypeStruct((rows, 2 * width), BF16),
        in_specs=[HBM_SPEC] * 2,
        out_specs=in_vmem(),
        scratch_shapes=[pltpu.SemaphoreType.DMA((2,))],
        compiler_params=LIMIT,
        name="side_by_side",
    )(in_hbm(left), in_hbm(right))


def add_and_cut(parts, sent, pieces):
    rows, width = sent[0].shape
    height = rows // pieces
    count = len(parts)

    def body(*refs):
        outs = refs[2 * count :]
        chunk = 1024
        for m in range(count):

            def step(n, carry):
                cols = pl.ds(pl.multiple_of(n * chunk, chunk), chunk)
                there = pl.ds(pl.multiple_of(m * width + n * chunk, chunk), chunk)
                total = refs[m][:, cols].astype(F32) + refs[count + m][:, cols].astype(F32)
                for i, out in enumerate(outs):
                    out[:, there] = total[i * height : (i + 1) * height].astype(BF16)
                return carry

            lax.fori_loop(0, width // chunk, step, 0)

    out = (jax.ShapeDtypeStruct((height, count * width), BF16),) * pieces
    return pl.pallas_call(
        body,
        out_shape=out,
        in_specs=[in_vmem()] * (2 * count),
        out_specs=(in_vmem(),) * pieces,
        compiler_params=LIMIT,
        cost_estimate=FREE,
        name="add_and_cut",
    )(*parts, *sent)


def scatter(index, blocks, dense, sem, first, count):
    size = blocks.shape[1]
    cols = dense.shape[1] // size
    scale = 2**16 // cols + 1
    for u in range(count):
        k = first + u
        b = index[0, k]
        r = lax.shift_right_logical(b * scale, 16)
        c = b - r * cols
        r, c = pl.multiple_of(r * size, size), pl.multiple_of(c * size, size)
        pltpu.make_async_copy(
            blocks.at[k], dense.at[pl.ds(r, size), pl.ds(c, size)], sem
        ).start()


def dense_body(again, index_hbm, blocks, *refs):
    if again:
        source, dense, copied, index, sem = refs[0], *refs[-4:]
        copy = pltpu.make_async_copy(source, copied, sem.at[2])
        copy.start()
    else:
        dense, index, sem = refs[-3:]
    fetch = pltpu.make_async_copy(index_hbm, index, sem.at[1])
    fetch.start()
    dense[...] = jnp.zeros_like(dense)
    fetch.wait()
    kept = blocks.shape[0]
    unroll = 8 if kept % 8 == 0 else 1

    def step(i, carry):
        scatter(index, blocks, dense, sem.at[0], i * unroll, unroll)
        return carry

    lax.fori_loop(0, kept // unroll, step, 0)
    if again:
        copy.wait()
    pltpu.make_async_copy(blocks, blocks, sem.at[0]).wait()


def dense(index, blocks, source, width, hidden, limit, wait_for=()):
    again = [] if source is None else [source]
    outs = [VMEM((width, hidden), BF16)] + [VMEM(x.shape, x.dtype) for x in again]
    return pl.pallas_call(
        functools.partial(dense_body, bool(again)),
        out_shape=outs,
        in_specs=[HBM_SPEC] * 2 + [ANY_SPEC] * (len(again) + len(wait_for)),
        out_specs=[in_vmem()] * len(outs),
        scratch_shapes=[pltpu.SMEM(index.shape, jnp.int32), pltpu.SemaphoreType.DMA((3,))],
        compiler_params=pltpu.CompilerParams(vmem_limit_bytes=limit),
        cost_estimate=FREE,
        name="dense",
    )(in_hbm(index), in_hbm(blocks), *again, *wait_for)


def chunk_of(hidden):
    return 256 if hidden % 256 == 0 else 128


def activations(tok, cot, wg, wu, wd):
    g = dot_nn(tok[...], wg)
    u = dot_nn(tok[...], wu)
    h = dot_nt(cot[...], wd)
    s = jax.nn.sigmoid(g)
    hid = (g * s * u).astype(BF16)
    gp = (h * u * s * (1.0 + g * (1.0 - s))).astype(BF16)
    up = (h * g * s).astype(BF16)
    return hid, gp, up


def acts_body(count, *refs):
    pieces, (wg, wu, wd), (hid, gp, up, x) = refs[:count], refs[count : count + 3], refs[-4:]
    n = pl.program_id(0)
    width, chunk = wg.shape[0], wd.shape[0]

    @pl.when(n == 0)
    def _():
        assemble(pieces, x)

    cols = pl.ds(pl.multiple_of(n * chunk, chunk), chunk)
    tok, cot = x.at[:, pl.ds(0, width)], x.at[:, pl.ds(width, width)]
    hid[...], gp[...], up[...] = activations(tok, cot, wg[:, cols], wu[:, cols], wd[...])


def acts_pass(pieces, wg, wu, wd, name, wait_for=()):
    rows = sum(x.shape[0] for x in pieces)
    width, hidden = wg.shape
    chunk = chunk_of(hidden)
    act = jax.ShapeDtypeStruct((rows, hidden), BF16)
    piece = pl.BlockSpec((rows, chunk), lambda n: (0, n))
    need = 84 * rows * chunk + 4 * chunk * width
    return pl.pallas_call(
        functools.partial(acts_body, len(pieces)),
        out_shape=(act, act, act, VMEM((rows, 2 * width), BF16)),
        grid=(hidden // chunk,),
        in_specs=[in_vmem()] * (len(pieces) + 2)
        + [pl.BlockSpec((chunk, width), lambda n: (n, 0))]
        + [ANY_SPEC] * len(wait_for),
        out_specs=(piece, piece, piece, in_vmem()),
        compiler_params=pltpu.CompilerParams(vmem_limit_bytes=max(need, 8 * 2**20)),
        cost_estimate=pl.CostEstimate(
            flops=6 * rows * width * hidden, bytes_accessed=2 * width * hidden, transcendentals=0
        ),
        name=name,
    )(*pieces, *pinned(wg, wu), in_hbm(wd), *wait_for)


def own_body(count, index_hbm, *refs):
    pieces, (wg, wu, blocks), refs = refs[:count], refs[count : count + 3], refs[count + 3 :]
    hid, gp, up, x, part, back, wd_out, wd, g_all, u_all, index, sem = refs
    width, hidden = wg.shape
    steps, _, chunk = g_all.shape
    kept = blocks.shape[0]
    each = kept // steps
    fetch = pltpu.make_async_copy(index_hbm, index, sem.at[1])
    fetch.start()
    assemble(pieces, x)

    def place(n):
        return pl.ds(pl.multiple_of(n * chunk, chunk), chunk)

    def gate(n, carry):
        g_all[n] = dot_nn(x[:, :width], wg[:, place(n)])
        wd[place(n)] = jnp.zeros((chunk, width), BF16)
        return carry

    lax.fori_loop(0, steps, gate, 0)
    fetch.wait()

    def up_proj(n, carry):
        scatter(index, blocks, wd, sem.at[0], n * each, each)
        u_all[n] = dot_nn(x[:, :width], wu[:, place(n)])
        return carry

    lax.fori_loop(0, steps, up_proj, 0)
    scatter(index, blocks, wd, sem.at[0], steps * each, kept - steps * each)
    pltpu.make_async_copy(blocks, blocks, sem.at[0]).wait()
    store = pltpu.make_async_copy(wd, wd_out, sem.at[2])
    store.start()

    def grad(n, carry):
        cols = place(n)
        g, u = g_all[n], u_all[n]
        h = dot_nt(x[:, width:], wd[cols])
        s = jax.nn.sigmoid(g)
        hid[:, cols] = (g * s * u).astype(BF16)
        gp[:, cols] = (h * u * s * (1.0 + g * (1.0 - s))).astype(BF16)
        up[:, cols] = (h * g * s).astype(BF16)
        return carry

    lax.fori_loop(0, steps, grad, 0)
    half = part.shape[0]
    wide = 1024

    def sums(n, carry):
        out = pl.ds(pl.multiple_of(n * wide, wide), wide)
        later = pl.ds(pl.multiple_of(width + n * wide, wide), wide)
        left = dot_nn(hid[...], wd[:, out]).astype(BF16)
        right = (dot_nt(gp[...], wg[out, :]) + dot_nt(up[...], wu[out, :])).astype(BF16)
        part[:, out] = left[:half]
        back[:, out] = left[half:]
        part[:, later] = right[:half]
        back[:, later] = right[half:]
        return carry

    lax.fori_loop(0, width // wide, sums, 0)
    store.wait()


def own_pass(pieces, wg, wu, index, blocks, limit):
    rows = sum(x.shape[0] for x in pieces)
    width, hidden = wg.shape
    chunk = chunk_of(hidden)
    act = VMEM((rows, hidden), BF16)
    half = VMEM((rows // 2, 2 * width), BF16)
    kept = VMEM((hidden // chunk, rows, chunk), F32)
    return pl.pallas_call(
        functools.partial(own_body, len(pieces)),
        out_shape=(
            act, act, act, VMEM((rows, 2 * width), BF16), half, half,
            pltpu.HBM((hidden, width), BF16),
        ),
        in_specs=[HBM_SPEC] + [in_vmem()] * (len(pieces) + 2) + [HBM_SPEC],
        out_specs=(in_vmem(),) * 6 + (HBM_SPEC,),
        scratch_shapes=[
            VMEM((hidden, width), BF16),
            kept,
            kept,
            pltpu.SMEM(index.shape, jnp.int32),
            pltpu.SemaphoreType.DMA((3,)),
        ],
        compiler_params=pltpu.CompilerParams(vmem_limit_bytes=limit),
        cost_estimate=pl.CostEstimate(
            flops=12 * rows * width * hidden, bytes_accessed=2 * width * hidden, transcendentals=0
        ),
        name="own_pass",
    )(in_hbm(index), *pieces, *pinned(wg, wu), in_hbm(blocks))


def grads_body(
    factor, size, group, spots, own, rest, hid0, hid1, gp0, gp1, up0, up1,
    gate_out, up_out, down_out, tok_t, hid_t, gate_buf, up_buf, down_buf, sem,
):
    cap = spots.shape[1]
    groups = cap // group
    d_cols = tok_t.shape[0]
    ff_cols = hid_t.shape[0]
    width = d_cols * size

    def column(first, second, start):
        cols = pl.ds(pl.multiple_of(start, size), size)
        return jnp.concatenate([first[:, cols], second[:, cols]], axis=0)

    def one(which, left, first, second, base, buf, cols, slot):
        spot = spots[which, slot]
        b = jnp.maximum(spot, 0)
        r = lax.shift_right_logical(b * (2**16 // cols + 1), 16)
        c = b - r * cols
        value = dot_nn(left[r], column(first, second, base + c * size)) * factor
        buf[slot] = jnp.where(spot >= 0, value, 0.0)

    def send(buf, out, slot, i):
        part = pl.ds(i * group, group)
        pltpu.make_async_copy(buf.at[part], out.at[part], sem.at[slot]).start()

    def turn_hidden(n, carry):
        hid_t[n] = column(hid0, hid1, n * size).T
        return carry

    lax.fori_loop(0, ff_cols, turn_hidden, 0)
    turns = -(-d_cols // groups)

    def down_step(i, carry):
        for j in range(max(group, turns)):
            if j < turns:
                n = jnp.minimum(i * turns + j, d_cols - 1)
                tok_t[n] = column(own, rest, n * size).T
            if j < group:
                one(2, hid_t, own, rest, width, down_buf, d_cols, i * group + j)
        send(down_buf, down_out, 2, i)
        return carry

    lax.fori_loop(0, groups, down_step, 0)

    def step(i, carry):
        for j in range(group):
            one(0, tok_t, gp0, gp1, 0, gate_buf, ff_cols, i * group + j)
            one(1, tok_t, up0, up1, 0, up_buf, ff_cols, i * group + j)
        send(gate_buf, gate_out, 0, i)
        send(up_buf, up_out, 1, i)
        return carry

    lax.fori_loop(0, groups, step, 0)
    for slot, (buf, out) in enumerate(((gate_buf, gate_out), (up_buf, up_out), (down_buf, down_out))):
        pltpu.make_async_copy(buf, out, sem.at[slot]).wait()


def grads(spots, own, rest, acts0, acts1, size, cap, factor):
    group = max(n for n in range(1, 18) if cap % n == 0)
    width = own.shape[1] // 2
    hidden = acts0[0].shape[1]
    rows = own.shape[0] + rest.shape[0]
    out = jax.ShapeDtypeStruct((cap, size, size), F32)
    buf = VMEM((cap, size, size), F32)
    need = rows * (6 * width + 8 * hidden) + cap * 12 * size * size
    return pl.pallas_call(
        functools.partial(grads_body, factor, size, group),
        out_shape=(out, out, out),
        in_specs=[SMEM_SPEC] + [in_vmem()] * 8,
        out_specs=(HBM_SPEC,) * 3,
        scratch_shapes=[
            VMEM((width // size, size, rows), BF16),
            VMEM((hidden // size, size, rows), BF16),
            buf,
            buf,
            buf,
            pltpu.SemaphoreType.DMA((3,)),
        ],
        compiler_params=pltpu.CompilerParams(vmem_limit_bytes=need + 2**21),
        cost_estimate=pl.CostEstimate(
            flops=6 * cap * size * size * rows, bytes_accessed=12 * cap * size * size, transcendentals=0
        ),
        name="grads",
    )(spots, own, rest, acts0[0], acts1[0], acts0[1], acts1[1], acts0[2], acts1[2])


def local(
    tokens,
    out_grad,
    gate_blocks,
    up_blocks,
    down_blocks,
    gate_index,
    up_index,
    down_index,
    gate_slot,
    up_slot,
    down_slot,
):
    rows, width = tokens.shape
    size = gate_blocks.shape[1]
    kept_count = gate_blocks.shape[0]
    groups = lax.axis_size("dp")
    slices = lax.axis_size("tensor")
    hidden = FF // slices
    cap = (kept_count + groups - 1) // groups + kept_count // (4 * groups)
    factor = 1.0 / math.sqrt(rows * slices * groups)

    mine = lax.axis_index("dp") * cap + jnp.arange(cap, dtype=jnp.int32)
    slots = jnp.concatenate([gate_slot, up_slot, down_slot])
    index = jnp.concatenate([gate_index, up_index, down_index])
    hit = slots[:, None, :] == mine[None, :, None]
    spots = jnp.sum(jnp.where(hit, index[:, None, :] + 1, 0), axis=2) - 1

    both = side_by_side(tokens, out_grad)
    chips = range(2, slices, 2)

    def sibling(x):
        return exchange(x, "tensor", 1)

    far = [exchange(both, "dp", a) for a in range(1, groups)]
    near = [exchange(both, "tensor", d) for d in chips[:-1]]
    stage = 2 * width * hidden
    wu, later = dense(up_index, up_blocks, both, width, hidden, DENSE_LIMIT)
    near.append(exchange(later, "tensor", chips[-1]))
    others = pack(far, [wu])
    (wg,) = dense(gate_index, gate_blocks, None, width, hidden, NEXT_LIMIT, [spots, others])
    own_half = pack([both, *near], [wg])
    own_pieces = [own_half, sibling(own_half)]
    other_half = [others, *(exchange(others, "tensor", d) for d in chips)]

    *acts0, own, part, back, wd = own_pass(
        own_pieces, wg, wu, down_index, down_blocks, stage + 3 * 2**20
    )
    chip = add_and_cut([part], [sibling(back)], slices // 2)
    acts1_in = [*other_half, *(sibling(x) for x in other_half)]
    *acts1, rest = acts_pass(acts1_in, wg, wu, wd, "rest_acts", [chip[0]])

    total = chip[0].astype(F32)
    for piece, d in zip(chip[1:], chips):
        total = total + exchange(piece, "tensor", d).astype(F32)
    total = total.astype(BF16)

    gate_out, up_out, down_out = grads(spots, own, rest, acts0, acts1, size, cap, factor)
    return (total[:, :width], total[:, width:], gate_out[None], up_out[None], down_out[None])


def solution(mesh):
    in_specs = (
        P(("dp", "tensor"), None),
        P(("dp", "tensor"), None),
        P("tensor", None, None),
        P("tensor", None, None),
        P("tensor", None, None),
        P("tensor", None),
        P("tensor", None),
        P("tensor", None),
        P("tensor", None),
        P("tensor", None),
        P("tensor", None),
    )
    out_specs = (
        P(("dp", "tensor"), None),
        P(("dp", "tensor"), None),
        P("tensor", "dp", None, None),
        P("tensor", "dp", None, None),
        P("tensor", "dp", None, None),
    )
    return jax.shard_map(local, mesh=mesh, in_specs=in_specs, out_specs=out_specs, check_vma=False)
```

```python
import functools
import math

import jax
import jax.numpy as jnp
from jax import lax
from jax.experimental import pallas as pl
from jax.experimental.pallas import tpu as pltpu
from jax.sharding import PartitionSpec as P

FF = 14336
BF16 = jnp.bfloat16
F32 = jnp.float32
VMEM = pltpu.VMEM
SMEM = pltpu.SMEM


SMEM_SPEC = pl.BlockSpec(memory_space=SMEM)
HBM_SPEC = pl.BlockSpec(memory_space=pltpu.HBM)
ANY_SPEC = pl.BlockSpec(memory_space=pl.ANY)
FREE = pl.CostEstimate(flops=0, bytes_accessed=0, transcendentals=0)
LIMIT = pltpu.CompilerParams(vmem_limit_bytes=4 * 2**20)
DENSE_LIMIT = 17 * 2**20
NEXT_LIMIT = 17 * 2**20


def in_vmem():
    return pl.BlockSpec(memory_space=VMEM)


def pinned(*arrays):
    return [pltpu.with_memory_space_constraint(x, VMEM) for x in arrays]


def in_hbm(x):
    return pltpu.with_memory_space_constraint(x, pltpu.HBM)


def dot_nn(a, b):
    return lax.dot_general(a, b, (((1,), (0,)), ((), ())), preferred_element_type=F32)


def dot_nt(a, b):
    return lax.dot_general(a, b, (((1,), (1,)), ((), ())), preferred_element_type=F32)


def exchange(x, axis, flip):
    count = lax.axis_size(axis)
    return lax.ppermute(x, axis, [(i, i ^ flip) for i in range(count)])


def assemble(pieces, out):
    chunk = 1024

    def step(n, carry):
        cols = pl.ds(pl.multiple_of(n * chunk, chunk), chunk)
        parts = [x[:, cols].astype(F32) for x in pieces]
        out[:, cols] = jnp.concatenate(parts, axis=0).astype(BF16)
        return carry

    lax.fori_loop(0, out.shape[1] // chunk, step, 0)


def pack(pieces, wait_for=()):
    rows = sum(x.shape[0] for x in pieces)
    width = pieces[0].shape[1]

    def body(*refs):
        assemble(refs[: len(pieces)], refs[-1])

    return pl.pallas_call(
        body,
        out_shape=jax.ShapeDtypeStruct((rows, width), BF16),
        in_specs=[in_vmem()] * len(pieces) + [ANY_SPEC] * len(wait_for),
        out_specs=in_vmem(),
        compiler_params=LIMIT,
        cost_estimate=FREE,
        name="pack",
    )(*pieces, *wait_for)


def side_by_side(left, right):
    rows, width = left.shape

    def body(left_ref, right_ref, out, sem):
        copies = [
            pltpu.make_async_copy(left_ref, out.at[:, pl.ds(0, width)], sem.at[0]),
            pltpu.make_async_copy(right_ref, out.at[:, pl.ds(width, width)], sem.at[1]),
        ]
        for copy in copies:
            copy.start()
        for copy in copies:
            copy.wait()

    return pl.pallas_call(
        body,
        out_shape=jax.ShapeDtypeStruct((rows, 2 * width), BF16),
        in_specs=[HBM_SPEC] * 2,
        out_specs=in_vmem(),
        scratch_shapes=[pltpu.SemaphoreType.DMA((2,))],
        compiler_params=LIMIT,
        name="side_by_side",
    )(in_hbm(left), in_hbm(right))


def add_and_cut(parts, sent, pieces):
    rows, width = sent[0].shape
    height = rows // pieces
    count = len(parts)

    def body(*refs):
        outs = refs[2 * count :]
        chunk = 1024
        for m in range(count):

            def step(n, carry):
                cols = pl.ds(pl.multiple_of(n * chunk, chunk), chunk)
                there = pl.ds(pl.multiple_of(m * width + n * chunk, chunk), chunk)
                total = refs[m][:, cols].astype(F32) + refs[count + m][:, cols].astype(F32)
                for i, out in enumerate(outs):
                    out[:, there] = total[i * height : (i + 1) * height].astype(BF16)
                return carry

            lax.fori_loop(0, width // chunk, step, 0)

    out = (jax.ShapeDtypeStruct((height, count * width), BF16),) * pieces
    return pl.pallas_call(
        body,
        out_shape=out,
        in_specs=[in_vmem()] * (2 * count),
        out_specs=(in_vmem(),) * pieces,
        compiler_params=LIMIT,
        cost_estimate=FREE,
        name="add_and_cut",
    )(*parts, *sent)


def scatter(index, blocks, dense, sem, first, count):
    size = blocks.shape[1]
    cols = dense.shape[1] // size
    scale = 2**16 // cols + 1
    for u in range(count):
        k = first + u
        b = index[0, k]
        r = lax.shift_right_logical(b * scale, 16)
        c = b - r * cols
        r, c = pl.multiple_of(r * size, size), pl.multiple_of(c * size, size)
        pltpu.make_async_copy(
            blocks.at[k], dense.at[pl.ds(r, size), pl.ds(c, size)], sem
        ).start()


def dense_body(index_hbm, blocks, *refs):
    dense, index, sem = refs[-3:]
    fetch = pltpu.make_async_copy(index_hbm, index, sem.at[1])
    fetch.start()
    dense[...] = jnp.zeros_like(dense)
    fetch.wait()
    fill_dense(index, blocks, dense, sem.at[0])
    pltpu.make_async_copy(blocks, blocks, sem.at[0]).wait()


def fill_dense(index, blocks, dense, sem):
    kept = blocks.shape[0]
    unroll = 8 if kept % 8 == 0 else 1

    def step(i, carry):
        scatter(index, blocks, dense, sem, i * unroll, unroll)
        return carry

    lax.fori_loop(0, kept // unroll, step, 0)


def dense_first_body(cap, index_hbm, blocks, source, *refs):
    lists, (dense, copied, spots, index, rows, sem) = refs[:6], refs[6:]
    copy = pltpu.make_async_copy(source, copied, sem.at[2])
    copy.start()
    fetch = pltpu.make_async_copy(index_hbm, index, sem.at[1])
    fetch.start()
    for n, ref in enumerate(lists):
        pltpu.make_async_copy(ref, rows.at[n], sem.at[3]).start()
    dense[...] = jnp.zeros_like(dense)
    fetch.wait()
    fill_dense(index, blocks, dense, sem.at[0])
    pltpu.make_async_copy(rows, rows, sem.at[3]).wait()
    kept = rows.shape[2]
    room = spots.shape[1]
    mine = lax.axis_index("dp") * cap + lax.broadcasted_iota(jnp.int32, (room, kept), 0)
    for n in range(3):
        held = jnp.where(rows[n] == mine, rows[3 + n] + 1, 0)
        found = jnp.sum(held, axis=1, keepdims=True) - 1
        spots[n : n + 1] = jnp.broadcast_to(found, (room, 128)).T[:1]
    copy.wait()
    pltpu.make_async_copy(blocks, blocks, sem.at[0]).wait()


def dense_first(index, blocks, source, slots, indexes, cap, width, hidden, limit):
    return pl.pallas_call(
        functools.partial(dense_first_body, cap),
        out_shape=(
            VMEM((width, hidden), BF16),
            VMEM(source.shape, source.dtype),
            jax.ShapeDtypeStruct((3, -(-cap // 128) * 128), jnp.int32),
        ),
        in_specs=[HBM_SPEC] * 2 + [ANY_SPEC] + [HBM_SPEC] * 6,
        out_specs=(in_vmem(),) * 3,
        scratch_shapes=[
            pltpu.SMEM(index.shape, jnp.int32),
            VMEM((6, *index.shape), jnp.int32),
            pltpu.SemaphoreType.DMA((4,)),
        ],
        compiler_params=pltpu.CompilerParams(vmem_limit_bytes=limit),
        cost_estimate=FREE,
        name="dense_first",
    )(in_hbm(index), in_hbm(blocks), source, *(in_hbm(x) for x in (*slots, *indexes)))


def dense(index, blocks, width, hidden, limit, wait_for):
    return pl.pallas_call(
        dense_body,
        out_shape=VMEM((width, hidden), BF16),
        in_specs=[HBM_SPEC] * 2 + [ANY_SPEC] * len(wait_for),
        out_specs=in_vmem(),
        scratch_shapes=[pltpu.SMEM(index.shape, jnp.int32), pltpu.SemaphoreType.DMA((2,))],
        compiler_params=pltpu.CompilerParams(vmem_limit_bytes=limit),
        cost_estimate=FREE,
        name="dense",
    )(in_hbm(index), in_hbm(blocks), *wait_for)


def chunk_of(hidden):
    return 256 if hidden % 256 == 0 else 128


def acts_body(count, *refs):
    pieces, (wg, wu, wd_hbm), refs = refs[:count], refs[count : count + 3], refs[count + 3 :]
    hid, gp, up, x, wd, sem = refs[-6:]
    width, hidden = wg.shape
    chunk = wd.shape[1]
    steps = hidden // chunk

    def place(n):
        return pl.ds(pl.multiple_of(n * chunk, chunk), chunk)

    def fetch(n):
        slot = lax.rem(n, 2)
        return pltpu.make_async_copy(wd_hbm.at[place(n)], wd.at[slot], sem.at[slot])

    fetch(0).start()
    assemble(pieces, x)

    def step(n, carry):
        @pl.when(n + 1 < steps)
        def _():
            fetch(n + 1).start()

        cols = place(n)
        g = dot_nn(x[:, :width], wg[:, cols])
        u = dot_nn(x[:, :width], wu[:, cols])
        fetch(n).wait()
        h = dot_nt(x[:, width:], wd[lax.rem(n, 2)])
        s = jax.nn.sigmoid(g)
        hid[:, cols] = (g * s * u).astype(BF16)
        gp[:, cols] = (h * u * s * (1.0 + g * (1.0 - s))).astype(BF16)
        up[:, cols] = (h * g * s).astype(BF16)
        return carry

    lax.fori_loop(0, steps, step, 0)


def acts_pass(pieces, wg, wu, wd, name, wait_for=()):
    rows = sum(x.shape[0] for x in pieces)
    width, hidden = wg.shape
    chunk = chunk_of(hidden)
    act = VMEM((rows, hidden), BF16)
    need = 84 * rows * chunk + 4 * chunk * width + 2**20 + (rows > 256) * 18 * 2**20
    return pl.pallas_call(
        functools.partial(acts_body, len(pieces)),
        out_shape=(act, act, act, VMEM((rows, 2 * width), BF16)),
        in_specs=[in_vmem()] * (len(pieces) + 2) + [HBM_SPEC] + [ANY_SPEC] * len(wait_for),
        out_specs=(in_vmem(),) * 4,
        scratch_shapes=[VMEM((2, chunk, width), BF16), pltpu.SemaphoreType.DMA((2,))],
        compiler_params=pltpu.CompilerParams(vmem_limit_bytes=max(need, 8 * 2**20)),
        cost_estimate=pl.CostEstimate(
            flops=6 * rows * width * hidden, bytes_accessed=2 * width * hidden, transcendentals=0
        ),
        name=name,
    )(*pieces, *pinned(wg, wu), in_hbm(wd), *wait_for)


def own_body(count, index_hbm, *refs):
    pieces, (wg, wu, blocks), refs = refs[:count], refs[count : count + 3], refs[count + 3 :]
    hid, gp, up, x, part, back, wd_out, wd, g_all, u_all, index, sem = refs
    width, hidden = wg.shape
    steps, _, chunk = g_all.shape
    kept = blocks.shape[0]
    each = kept // steps
    fetch = pltpu.make_async_copy(index_hbm, index, sem.at[1])
    fetch.start()
    assemble(pieces, x)

    def place(n):
        return pl.ds(pl.multiple_of(n * chunk, chunk), chunk)

    def gate(n, carry):
        g_all[n] = dot_nn(x[:, :width], wg[:, place(n)])
        wd[place(n)] = jnp.zeros((chunk, width), BF16)
        return carry

    lax.fori_loop(0, steps, gate, 0)
    fetch.wait()

    def up_proj(n, carry):
        scatter(index, blocks, wd, sem.at[0], n * each, each)
        u_all[n] = dot_nn(x[:, :width], wu[:, place(n)])
        return carry

    lax.fori_loop(0, steps, up_proj, 0)
    scatter(index, blocks, wd, sem.at[0], steps * each, kept - steps * each)
    pltpu.make_async_copy(blocks, blocks, sem.at[0]).wait()
    store = pltpu.make_async_copy(wd, wd_out, sem.at[2])
    store.start()

    def grad(n, carry):
        cols = place(n)
        g, u = g_all[n], u_all[n]
        h = dot_nt(x[:, width:], wd[cols])
        s = jax.nn.sigmoid(g)
        hid[:, cols] = (g * s * u).astype(BF16)
        gp[:, cols] = (h * u * s * (1.0 + g * (1.0 - s))).astype(BF16)
        up[:, cols] = (h * g * s).astype(BF16)
        return carry

    lax.fori_loop(0, steps, grad, 0)
    half = part.shape[0]
    wide = 1024

    def sums(n, carry):
        out = pl.ds(pl.multiple_of(n * wide, wide), wide)
        later = pl.ds(pl.multiple_of(width + n * wide, wide), wide)
        left = dot_nn(hid[...], wd[:, out]).astype(BF16)
        right = (dot_nt(gp[...], wg[out, :]) + dot_nt(up[...], wu[out, :])).astype(BF16)
        part[:, out] = left[:half]
        back[:, out] = left[half:]
        part[:, later] = right[:half]
        back[:, later] = right[half:]
        return carry

    lax.fori_loop(0, width // wide, sums, 0)
    store.wait()


def own_pass(pieces, wg, wu, index, blocks, limit):
    rows = sum(x.shape[0] for x in pieces)
    width, hidden = wg.shape
    chunk = chunk_of(hidden)
    act = VMEM((rows, hidden), BF16)
    half = VMEM((rows // 2, 2 * width), BF16)
    kept = VMEM((hidden // chunk, rows, chunk), F32)
    return pl.pallas_call(
        functools.partial(own_body, len(pieces)),
        out_shape=(
            act, act, act, VMEM((rows, 2 * width), BF16), half, half,
            pltpu.HBM((hidden, width), BF16),
        ),
        in_specs=[HBM_SPEC] + [in_vmem()] * (len(pieces) + 2) + [HBM_SPEC],
        out_specs=(in_vmem(),) * 6 + (HBM_SPEC,),
        scratch_shapes=[
            VMEM((hidden, width), BF16),
            kept,
            kept,
            pltpu.SMEM(index.shape, jnp.int32),
            pltpu.SemaphoreType.DMA((3,)),
        ],
        compiler_params=pltpu.CompilerParams(vmem_limit_bytes=limit),
        cost_estimate=pl.CostEstimate(
            flops=12 * rows * width * hidden, bytes_accessed=2 * width * hidden, transcendentals=0
        ),
        name="own_pass",
    )(in_hbm(index), *pieces, *pinned(wg, wu), in_hbm(blocks))


def grads_body(
    factor, size, group, spots, own, rest, hid0, hid1, gp0, gp1, up0, up1, *refs
):
    sums = refs[:-11]
    layer, token_grad, gate_out, up_out, down_out = refs[-11:-6]
    tok_t, hid_t, gate_buf, up_buf, down_buf, sem = refs[-6:]
    cap = gate_buf.shape[0]
    groups = cap // group
    d_cols = tok_t.shape[0]
    ff_cols = hid_t.shape[0]
    width = d_cols * size

    def column(first, second, start):
        cols = pl.ds(pl.multiple_of(start, size), size)
        return jnp.concatenate([first[:, cols], second[:, cols]], axis=0)

    def one(which, left, first, second, base, buf, cols, slot):
        spot = spots[which, slot]
        b = jnp.maximum(spot, 0)
        r = lax.shift_right_logical(b * (2**16 // cols + 1), 16)
        c = b - r * cols
        value = dot_nn(left[r], column(first, second, base + c * size)) * factor
        buf[slot] = jnp.where(spot >= 0, value, 0.0)

    def send(buf, out, slot, i):
        part = pl.ds(i * group, group)
        pltpu.make_async_copy(buf.at[part], out.at[part], sem.at[slot]).start()

    def last_sum(n, carry):
        chunk = 1024
        for out, base in ((layer, 0), (token_grad, width)):
            cols = pl.ds(pl.multiple_of(n * chunk, chunk), chunk)
            there = pl.ds(pl.multiple_of(base + n * chunk, chunk), chunk)
            total = sums[0][:, there].astype(F32)
            for piece in sums[1:]:
                total = total + piece[:, there].astype(F32)
            out[:, cols] = total.astype(BF16)
        return carry

    lax.fori_loop(0, width // 1024, last_sum, 0)

    def turn_hidden(n, carry):
        hid_t[n] = column(hid0, hid1, n * size).T
        return carry

    lax.fori_loop(0, ff_cols, turn_hidden, 0)
    turns = -(-d_cols // groups)

    def down_step(i, carry):
        for j in range(max(group, turns)):
            if j < turns:
                n = jnp.minimum(i * turns + j, d_cols - 1)
                tok_t[n] = column(own, rest, n * size).T
            if j < group:
                one(2, hid_t, own, rest, width, down_buf, d_cols, i * group + j)
        send(down_buf, down_out, 2, i)
        return carry

    lax.fori_loop(0, groups, down_step, 0)

    def step(i, carry):
        for j in range(group):
            one(0, tok_t, gp0, gp1, 0, gate_buf, ff_cols, i * group + j)
            one(1, tok_t, up0, up1, 0, up_buf, ff_cols, i * group + j)
        send(gate_buf, gate_out, 0, i)
        send(up_buf, up_out, 1, i)
        return carry

    lax.fori_loop(0, groups, step, 0)
    for slot, (buf, out) in enumerate(((gate_buf, gate_out), (up_buf, up_out), (down_buf, down_out))):
        pltpu.make_async_copy(buf, out, sem.at[slot]).wait()


def grads(spots, own, rest, acts0, acts1, sums, size, cap, factor):
    group = max(n for n in range(1, 18) if cap % n == 0)
    width = own.shape[1] // 2
    hidden = acts0[0].shape[1]
    rows = own.shape[0] + rest.shape[0]
    out = jax.ShapeDtypeStruct((cap, size, size), F32)
    buf = VMEM((cap, size, size), F32)
    need = rows * (6 * width + 8 * hidden) + cap * 12 * size * size
    return pl.pallas_call(
        functools.partial(grads_body, factor, size, group),
        out_shape=(jax.ShapeDtypeStruct((sums[0].shape[0], width), BF16),) * 2 + (out, out, out),
        in_specs=[SMEM_SPEC] + [in_vmem()] * (8 + len(sums)),
        out_specs=(in_vmem(),) * 2 + (HBM_SPEC,) * 3,
        scratch_shapes=[
            VMEM((width // size, size, rows), BF16),
            VMEM((hidden // size, size, rows), BF16),
            buf,
            buf,
            buf,
            pltpu.SemaphoreType.DMA((3,)),
        ],
        compiler_params=pltpu.CompilerParams(vmem_limit_bytes=need + 2**21),
        cost_estimate=pl.CostEstimate(
            flops=6 * cap * size * size * rows, bytes_accessed=12 * cap * size * size, transcendentals=0
        ),
        name="grads",
    )(spots, own, rest, acts0[0], acts1[0], acts0[1], acts1[1], acts0[2], acts1[2], *sums)


def local(
    tokens,
    out_grad,
    gate_blocks,
    up_blocks,
    down_blocks,
    gate_index,
    up_index,
    down_index,
    gate_slot,
    up_slot,
    down_slot,
):
    rows, width = tokens.shape
    size = gate_blocks.shape[1]
    kept_count = gate_blocks.shape[0]
    groups = lax.axis_size("dp")
    slices = lax.axis_size("tensor")
    hidden = FF // slices
    cap = (kept_count + groups - 1) // groups + kept_count // (4 * groups)
    factor = 1.0 / math.sqrt(rows * slices * groups)

    both = side_by_side(tokens, out_grad)
    chips = range(2, slices, 2)

    def sibling(x):
        return exchange(x, "tensor", 1)

    far = [exchange(both, "dp", a) for a in range(1, groups)]
    near = [exchange(both, "tensor", d) for d in chips[:-1]]
    stage = 2 * width * hidden
    wu, later, spots = dense_first(
        up_index,
        up_blocks,
        both,
        (gate_slot, up_slot, down_slot),
        (gate_index, up_index, down_index),
        cap,
        width,
        hidden,
        DENSE_LIMIT,
    )
    near.append(exchange(later, "tensor", chips[-1]))
    others = pack(far, [wu])
    wg = dense(gate_index, gate_blocks, width, hidden, NEXT_LIMIT, [others])
    own_half = pack([both, *near], [wg])
    own_pieces = [own_half, sibling(own_half)]
    other_half = [others, *(exchange(others, "tensor", d) for d in chips)]

    *acts0, own, part, back, wd = own_pass(
        own_pieces, wg, wu, down_index, down_blocks, stage + 3 * 2**20
    )
    chip = add_and_cut([part], [sibling(back)], slices // 2)
    acts1_in = [*other_half, *(sibling(x) for x in other_half)]
    *acts1, rest = acts_pass(acts1_in, wg, wu, wd, "rest_acts", [chip[0]])

    sums = [chip[0], *(exchange(piece, "tensor", d) for piece, d in zip(chip[1:], chips))]
    layer_out, token_grad, gate_out, up_out, down_out = grads(
        spots, own, rest, acts0, acts1, sums, size, cap, factor
    )
    return (layer_out, token_grad, gate_out[None], up_out[None], down_out[None])


def solution(mesh):
    in_specs = (
        P(("dp", "tensor"), None),
        P(("dp", "tensor"), None),
        P("tensor", None, None),
        P("tensor", None, None),
        P("tensor", None, None),
        P("tensor", None),
        P("tensor", None),
        P("tensor", None),
        P("tensor", None),
        P("tensor", None),
        P("tensor", None),
    )
    out_specs = (
        P(("dp", "tensor"), None),
        P(("dp", "tensor"), None),
        P("tensor", "dp", None, None),
        P("tensor", "dp", None, None),
        P("tensor", "dp", None, None),
    )
    return jax.shard_map(local, mesh=mesh, in_specs=in_specs, out_specs=out_specs, check_vma=False)
```

```python
import functools
import math

import jax
import jax.numpy as jnp
from jax import lax
from jax.experimental import pallas as pl
from jax.experimental.pallas import tpu as pltpu
from jax.sharding import PartitionSpec as P

FF = 14336
BF16 = jnp.bfloat16
F32 = jnp.float32
VMEM = pltpu.VMEM
SMEM = pltpu.SMEM


SMEM_SPEC = pl.BlockSpec(memory_space=SMEM)
HBM_SPEC = pl.BlockSpec(memory_space=pltpu.HBM)
ANY_SPEC = pl.BlockSpec(memory_space=pl.ANY)
FREE = pl.CostEstimate(flops=0, bytes_accessed=0, transcendentals=0)
LIMIT = pltpu.CompilerParams(vmem_limit_bytes=4 * 2**20)
DENSE_LIMIT = 17 * 2**20
NEXT_LIMIT = 17 * 2**20


def in_vmem():
    return pl.BlockSpec(memory_space=VMEM)


def pinned(*arrays):
    return [pltpu.with_memory_space_constraint(x, VMEM) for x in arrays]


def in_hbm(x):
    return pltpu.with_memory_space_constraint(x, pltpu.HBM)


def dot_nn(a, b):
    return lax.dot_general(a, b, (((1,), (0,)), ((), ())), preferred_element_type=F32)


def dot_nt(a, b):
    return lax.dot_general(a, b, (((1,), (1,)), ((), ())), preferred_element_type=F32)


def exchange(x, axis, flip):
    count = lax.axis_size(axis)
    return lax.ppermute(x, axis, [(i, i ^ flip) for i in range(count)])


def assemble(pieces, out):
    chunk = 1024

    def step(n, carry):
        cols = pl.ds(pl.multiple_of(n * chunk, chunk), chunk)
        parts = [x[:, cols].astype(F32) for x in pieces]
        out[:, cols] = jnp.concatenate(parts, axis=0).astype(BF16)
        return carry

    lax.fori_loop(0, out.shape[1] // chunk, step, 0)


def pack(pieces, wait_for=()):
    rows = sum(x.shape[0] for x in pieces)
    width = pieces[0].shape[1]

    def body(*refs):
        assemble(refs[: len(pieces)], refs[-1])

    return pl.pallas_call(
        body,
        out_shape=jax.ShapeDtypeStruct((rows, width), BF16),
        in_specs=[in_vmem()] * len(pieces) + [ANY_SPEC] * len(wait_for),
        out_specs=in_vmem(),
        compiler_params=LIMIT,
        cost_estimate=FREE,
        name="pack",
    )(*pieces, *wait_for)


def side_by_side(left, right):
    rows, width = left.shape

    def body(left_ref, right_ref, out, sem):
        copies = [
            pltpu.make_async_copy(left_ref, out.at[:, pl.ds(0, width)], sem.at[0]),
            pltpu.make_async_copy(right_ref, out.at[:, pl.ds(width, width)], sem.at[1]),
        ]
        for copy in copies:
            copy.start()
        for copy in copies:
            copy.wait()

    return pl.pallas_call(
        body,
        out_shape=jax.ShapeDtypeStruct((rows, 2 * width), BF16),
        in_specs=[HBM_SPEC] * 2,
        out_specs=in_vmem(),
        scratch_shapes=[pltpu.SemaphoreType.DMA((2,))],
        compiler_params=LIMIT,
        name="side_by_side",
    )(in_hbm(left), in_hbm(right))


def add_and_cut(parts, sent, pieces):
    rows, width = sent[0].shape
    height = rows // pieces
    count = len(parts)

    def body(*refs):
        outs = refs[2 * count :]
        chunk = 1024
        for m in range(count):

            def step(n, carry):
                cols = pl.ds(pl.multiple_of(n * chunk, chunk), chunk)
                there = pl.ds(pl.multiple_of(m * width + n * chunk, chunk), chunk)
                total = refs[m][:, cols].astype(F32) + refs[count + m][:, cols].astype(F32)
                for i, out in enumerate(outs):
                    out[:, there] = total[i * height : (i + 1) * height].astype(BF16)
                return carry

            lax.fori_loop(0, width // chunk, step, 0)

    out = (jax.ShapeDtypeStruct((height, count * width), BF16),) * pieces
    return pl.pallas_call(
        body,
        out_shape=out,
        in_specs=[in_vmem()] * (2 * count),
        out_specs=(in_vmem(),) * pieces,
        compiler_params=LIMIT,
        cost_estimate=FREE,
        name="add_and_cut",
    )(*parts, *sent)


def scatter(index, blocks, dense, sem, first, count):
    size = blocks.shape[1]
    cols = dense.shape[1] // size
    scale = 2**16 // cols + 1
    for u in range(count):
        k = first + u
        b = index[0, k]
        r = lax.shift_right_logical(b * scale, 16)
        c = b - r * cols
        r, c = pl.multiple_of(r * size, size), pl.multiple_of(c * size, size)
        pltpu.make_async_copy(
            blocks.at[k], dense.at[pl.ds(r, size), pl.ds(c, size)], sem
        ).start()


def dense_body(index_hbm, blocks, *refs):
    dense, index, sem = refs[-3:]
    fetch = pltpu.make_async_copy(index_hbm, index, sem.at[1])
    fetch.start()
    dense[...] = jnp.zeros_like(dense)
    fetch.wait()
    fill_dense(index, blocks, dense, sem.at[0])
    pltpu.make_async_copy(blocks, blocks, sem.at[0]).wait()


def fill_dense(index, blocks, dense, sem):
    kept = blocks.shape[0]
    unroll = 8 if kept % 8 == 0 else 1

    def step(i, carry):
        scatter(index, blocks, dense, sem, i * unroll, unroll)
        return carry

    lax.fori_loop(0, kept // unroll, step, 0)


def dense_first_body(cap, index_hbm, blocks, source, *refs):
    lists, (dense, copied, spots, index, rows, sem) = refs[:6], refs[6:]
    copy = pltpu.make_async_copy(source, copied, sem.at[2])
    copy.start()
    fetch = pltpu.make_async_copy(index_hbm, index, sem.at[1])
    fetch.start()
    for n, ref in enumerate(lists):
        pltpu.make_async_copy(ref, rows.at[n], sem.at[3]).start()
    dense[...] = jnp.zeros_like(dense)
    fetch.wait()
    fill_dense(index, blocks, dense, sem.at[0])
    pltpu.make_async_copy(rows, rows, sem.at[3]).wait()
    kept = rows.shape[2]
    room = spots.shape[1]
    mine = lax.axis_index("dp") * cap + lax.broadcasted_iota(jnp.int32, (room, kept), 0)
    for n in range(3):
        held = jnp.where(rows[n] == mine, rows[3 + n] + 1, 0)
        found = jnp.sum(held, axis=1, keepdims=True) - 1
        spots[n : n + 1] = jnp.broadcast_to(found, (room, 128)).T[:1]
    copy.wait()
    pltpu.make_async_copy(blocks, blocks, sem.at[0]).wait()


def dense_first(index, blocks, source, slots, indexes, cap, width, hidden, limit):
    return pl.pallas_call(
        functools.partial(dense_first_body, cap),
        out_shape=(
            VMEM((width, hidden), BF16),
            VMEM(source.shape, source.dtype),
            jax.ShapeDtypeStruct((3, -(-cap // 128) * 128), jnp.int32),
        ),
        in_specs=[HBM_SPEC] * 2 + [ANY_SPEC] + [HBM_SPEC] * 6,
        out_specs=(in_vmem(),) * 3,
        scratch_shapes=[
            pltpu.SMEM(index.shape, jnp.int32),
            VMEM((6, *index.shape), jnp.int32),
            pltpu.SemaphoreType.DMA((4,)),
        ],
        compiler_params=pltpu.CompilerParams(vmem_limit_bytes=limit),
        cost_estimate=FREE,
        name="dense_first",
    )(in_hbm(index), in_hbm(blocks), source, *(in_hbm(x) for x in (*slots, *indexes)))


def dense(index, blocks, width, hidden, limit, wait_for):
    return pl.pallas_call(
        dense_body,
        out_shape=VMEM((width, hidden), BF16),
        in_specs=[HBM_SPEC] * 2 + [ANY_SPEC] * len(wait_for),
        out_specs=in_vmem(),
        scratch_shapes=[pltpu.SMEM(index.shape, jnp.int32), pltpu.SemaphoreType.DMA((2,))],
        compiler_params=pltpu.CompilerParams(vmem_limit_bytes=limit),
        cost_estimate=FREE,
        name="dense",
    )(in_hbm(index), in_hbm(blocks), *wait_for)


def chunk_of(hidden):
    return 256 if hidden % 256 == 0 else 128


def broad_of(hidden):
    return 896 if hidden % 896 == 0 else 128


def acts_body(count, *refs):
    pieces, (wg, wu, wd_hbm), refs = refs[:count], refs[count : count + 3], refs[count + 3 :]
    hid, gp, up, x, wd, sem = refs[-6:]
    width, hidden = wg.shape
    chunk = wd.shape[1]
    steps = hidden // chunk

    def place(n):
        return pl.ds(pl.multiple_of(n * chunk, chunk), chunk)

    def fetch(n):
        slot = lax.rem(n, 2)
        return pltpu.make_async_copy(wd_hbm.at[place(n)], wd.at[slot], sem.at[slot])

    fetch(0).start()
    assemble(pieces, x)

    def step(n, carry):
        @pl.when(n + 1 < steps)
        def _():
            fetch(n + 1).start()

        cols = place(n)
        g = dot_nn(x[:, :width], wg[:, cols])
        u = dot_nn(x[:, :width], wu[:, cols])
        fetch(n).wait()
        h = dot_nt(x[:, width:], wd[lax.rem(n, 2)])
        s = jax.nn.sigmoid(g)
        hid[:, cols] = (g * s * u).astype(BF16)
        gp[:, cols] = (h * u * s * (1.0 + g * (1.0 - s))).astype(BF16)
        up[:, cols] = (h * g * s).astype(BF16)
        return carry

    lax.fori_loop(0, steps, step, 0)


def acts_pass(pieces, wg, wu, wd, name, wait_for=()):
    rows = sum(x.shape[0] for x in pieces)
    width, hidden = wg.shape
    chunk = chunk_of(hidden)
    act = VMEM((rows, hidden), BF16)
    need = 84 * rows * chunk + 4 * chunk * width + 2**20 + (rows > 256) * 18 * 2**20
    return pl.pallas_call(
        functools.partial(acts_body, len(pieces)),
        out_shape=(act, act, act, VMEM((rows, 2 * width), BF16)),
        in_specs=[in_vmem()] * (len(pieces) + 2) + [HBM_SPEC] + [ANY_SPEC] * len(wait_for),
        out_specs=(in_vmem(),) * 4,
        scratch_shapes=[VMEM((2, chunk, width), BF16), pltpu.SemaphoreType.DMA((2,))],
        compiler_params=pltpu.CompilerParams(vmem_limit_bytes=max(need, 8 * 2**20)),
        cost_estimate=pl.CostEstimate(
            flops=6 * rows * width * hidden, bytes_accessed=2 * width * hidden, transcendentals=0
        ),
        name=name,
    )(*pieces, *pinned(wg, wu), in_hbm(wd), *wait_for)


def own_body(count, index_hbm, *refs):
    pieces, (wg, wu, blocks), refs = refs[:count], refs[count : count + 3], refs[count + 3 :]
    hid, gp, up, x, part, back, wd_out, wd, g_all, u_all, index, sem = refs
    width, hidden = wg.shape
    chunk = chunk_of(hidden)
    steps = hidden // chunk
    fetch = pltpu.make_async_copy(index_hbm, index, sem.at[1])
    fetch.start()
    assemble(pieces, x)

    def place(n):
        return pl.ds(pl.multiple_of(n * chunk, chunk), chunk)

    broad = broad_of(hidden)

    def span(n):
        return pl.ds(pl.multiple_of(n * broad, 128), broad)

    def gate(n, carry):
        g_all[:, span(n)] = dot_nn(x[:, :width], wg[:, span(n)])
        wd[span(n)] = jnp.zeros((broad, width), BF16)
        return carry

    lax.fori_loop(0, hidden // broad, gate, 0)
    fetch.wait()
    fill_dense(index, blocks, wd, sem.at[0])

    def up_proj(n, carry):
        u_all[:, span(n)] = dot_nn(x[:, :width], wu[:, span(n)])
        return carry

    lax.fori_loop(0, hidden // broad, up_proj, 0)
    pltpu.make_async_copy(blocks, blocks, sem.at[0]).wait()
    store = pltpu.make_async_copy(wd, wd_out, sem.at[2])
    store.start()

    def grad(n, carry):
        cols = place(n)
        g, u = g_all[:, cols], u_all[:, cols]
        h = dot_nt(x[:, width:], wd[cols])
        s = jax.nn.sigmoid(g)
        hid[:, cols] = (g * s * u).astype(BF16)
        gp[:, cols] = (h * u * s * (1.0 + g * (1.0 - s))).astype(BF16)
        up[:, cols] = (h * g * s).astype(BF16)
        return carry

    lax.fori_loop(0, steps, grad, 0)
    half = part.shape[0]
    wide = 2048

    def sums(n, carry):
        out = pl.ds(pl.multiple_of(n * wide, wide), wide)
        later = pl.ds(pl.multiple_of(width + n * wide, wide), wide)
        left = dot_nn(hid[...], wd[:, out]).astype(BF16)
        right = (dot_nt(gp[...], wg[out, :]) + dot_nt(up[...], wu[out, :])).astype(BF16)
        part[:, out] = left[:half]
        back[:, out] = left[half:]
        part[:, later] = right[:half]
        back[:, later] = right[half:]
        return carry

    lax.fori_loop(0, width // wide, sums, 0)
    store.wait()


def own_pass(pieces, wg, wu, index, blocks, limit):
    rows = sum(x.shape[0] for x in pieces)
    width, hidden = wg.shape
    act = VMEM((rows, hidden), BF16)
    half = VMEM((rows // 2, 2 * width), BF16)
    kept = VMEM((rows, hidden), F32)
    return pl.pallas_call(
        functools.partial(own_body, len(pieces)),
        out_shape=(
            act, act, act, VMEM((rows, 2 * width), BF16), half, half,
            pltpu.HBM((hidden, width), BF16),
        ),
        in_specs=[HBM_SPEC] + [in_vmem()] * (len(pieces) + 2) + [HBM_SPEC],
        out_specs=(in_vmem(),) * 6 + (HBM_SPEC,),
        scratch_shapes=[
            VMEM((hidden, width), BF16),
            kept,
            kept,
            pltpu.SMEM(index.shape, jnp.int32),
            pltpu.SemaphoreType.DMA((3,)),
        ],
        compiler_params=pltpu.CompilerParams(vmem_limit_bytes=limit),
        cost_estimate=pl.CostEstimate(
            flops=12 * rows * width * hidden, bytes_accessed=2 * width * hidden, transcendentals=0
        ),
        name="own_pass",
    )(in_hbm(index), *pieces, *pinned(wg, wu), in_hbm(blocks))


def grads_body(
    factor, size, group, spots, own, rest, hid0, hid1, gp0, gp1, up0, up1, *refs
):
    sums = refs[:-11]
    layer, token_grad, gate_out, up_out, down_out = refs[-11:-6]
    tok_t, hid_t, gate_buf, up_buf, down_buf, sem = refs[-6:]
    cap = gate_buf.shape[0]
    groups = cap // group
    d_cols = tok_t.shape[0]
    ff_cols = hid_t.shape[0]
    width = d_cols * size

    def column(first, second, start):
        cols = pl.ds(pl.multiple_of(start, size), size)
        return jnp.concatenate([first[:, cols], second[:, cols]], axis=0)

    def one(which, left, first, second, base, buf, cols, slot):
        spot = spots[which, slot]
        b = jnp.maximum(spot, 0)
        r = lax.shift_right_logical(b * (2**16 // cols + 1), 16)
        c = b - r * cols
        value = dot_nn(left[r], column(first, second, base + c * size)) * factor
        buf[slot] = jnp.where(spot >= 0, value, 0.0)

    def send(buf, out, slot, i):
        part = pl.ds(i * group, group)
        pltpu.make_async_copy(buf.at[part], out.at[part], sem.at[slot]).start()

    def last_sum(n, carry):
        chunk = 1024
        for out, base in ((layer, 0), (token_grad, width)):
            cols = pl.ds(pl.multiple_of(n * chunk, chunk), chunk)
            there = pl.ds(pl.multiple_of(base + n * chunk, chunk), chunk)
            total = sums[0][:, there].astype(F32)
            for piece in sums[1:]:
                total = total + piece[:, there].astype(F32)
            out[:, cols] = total.astype(BF16)
        return carry

    lax.fori_loop(0, width // 1024, last_sum, 0)

    def turn_hidden(n, carry):
        hid_t[n] = column(hid0, hid1, n * size).T
        return carry

    lax.fori_loop(0, ff_cols, turn_hidden, 0)
    turns = -(-d_cols // groups)

    def down_step(i, carry):
        for j in range(max(group, turns)):
            if j < turns:
                n = jnp.minimum(i * turns + j, d_cols - 1)
                tok_t[n] = column(own, rest, n * size).T
            if j < group:
                one(2, hid_t, own, rest, width, down_buf, d_cols, i * group + j)
        send(down_buf, down_out, 2, i)
        return carry

    lax.fori_loop(0, groups, down_step, 0)

    def step(i, carry):
        for j in range(group):
            one(0, tok_t, gp0, gp1, 0, gate_buf, ff_cols, i * group + j)
            one(1, tok_t, up0, up1, 0, up_buf, ff_cols, i * group + j)
        send(gate_buf, gate_out, 0, i)
        send(up_buf, up_out, 1, i)
        return carry

    lax.fori_loop(0, groups, step, 0)
    for slot, (buf, out) in enumerate(((gate_buf, gate_out), (up_buf, up_out), (down_buf, down_out))):
        pltpu.make_async_copy(buf, out, sem.at[slot]).wait()


def grads(spots, own, rest, acts0, acts1, sums, size, cap, factor):
    group = max(n for n in range(1, 18) if cap % n == 0)
    width = own.shape[1] // 2
    hidden = acts0[0].shape[1]
    rows = own.shape[0] + rest.shape[0]
    out = jax.ShapeDtypeStruct((cap, size, size), F32)
    buf = VMEM((cap, size, size), F32)
    need = rows * (6 * width + 8 * hidden) + cap * 12 * size * size
    return pl.pallas_call(
        functools.partial(grads_body, factor, size, group),
        out_shape=(jax.ShapeDtypeStruct((sums[0].shape[0], width), BF16),) * 2 + (out, out, out),
        in_specs=[SMEM_SPEC] + [in_vmem()] * (8 + len(sums)),
        out_specs=(in_vmem(),) * 2 + (HBM_SPEC,) * 3,
        scratch_shapes=[
            VMEM((width // size, size, rows), BF16),
            VMEM((hidden // size, size, rows), BF16),
            buf,
            buf,
            buf,
            pltpu.SemaphoreType.DMA((3,)),
        ],
        compiler_params=pltpu.CompilerParams(vmem_limit_bytes=need + 2**21),
        cost_estimate=pl.CostEstimate(
            flops=6 * cap * size * size * rows, bytes_accessed=12 * cap * size * size, transcendentals=0
        ),
        name="grads",
    )(spots, own, rest, acts0[0], acts1[0], acts0[1], acts1[1], acts0[2], acts1[2], *sums)


def local(
    tokens,
    out_grad,
    gate_blocks,
    up_blocks,
    down_blocks,
    gate_index,
    up_index,
    down_index,
    gate_slot,
    up_slot,
    down_slot,
):
    rows, width = tokens.shape
    size = gate_blocks.shape[1]
    kept_count = gate_blocks.shape[0]
    groups = lax.axis_size("dp")
    slices = lax.axis_size("tensor")
    hidden = FF // slices
    cap = (kept_count + groups - 1) // groups + kept_count // (4 * groups)
    factor = 1.0 / math.sqrt(rows * slices * groups)

    both = side_by_side(tokens, out_grad)
    chips = range(2, slices, 2)

    def sibling(x):
        return exchange(x, "tensor", 1)

    far = [exchange(both, "dp", a) for a in range(1, groups)]
    near = [exchange(both, "tensor", d) for d in chips[:-1]]
    stage = 2 * width * hidden
    wu, later, spots = dense_first(
        up_index,
        up_blocks,
        both,
        (gate_slot, up_slot, down_slot),
        (gate_index, up_index, down_index),
        cap,
        width,
        hidden,
        DENSE_LIMIT,
    )
    near.append(exchange(later, "tensor", chips[-1]))
    others = pack(far, [wu])
    wg = dense(gate_index, gate_blocks, width, hidden, NEXT_LIMIT, [others])
    own_half = pack([both, *near], [wg])
    own_pieces = [own_half, sibling(own_half)]
    other_half = [others, *(exchange(others, "tensor", d) for d in chips)]

    *acts0, own, part, back, wd = own_pass(
        own_pieces, wg, wu, down_index, down_blocks, stage + 3 * 2**20
    )
    chip = add_and_cut([part], [sibling(back)], slices // 2)
    acts1_in = [*other_half, *(sibling(x) for x in other_half)]
    *acts1, rest = acts_pass(acts1_in, wg, wu, wd, "rest_acts", [chip[0]])

    sums = [chip[0], *(exchange(piece, "tensor", d) for piece, d in zip(chip[1:], chips))]
    layer_out, token_grad, gate_out, up_out, down_out = grads(
        spots, own, rest, acts0, acts1, sums, size, cap, factor
    )
    return (layer_out, token_grad, gate_out[None], up_out[None], down_out[None])


def solution(mesh):
    in_specs = (
        P(("dp", "tensor"), None),
        P(("dp", "tensor"), None),
        P("tensor", None, None),
        P("tensor", None, None),
        P("tensor", None, None),
        P("tensor", None),
        P("tensor", None),
        P("tensor", None),
        P("tensor", None),
        P("tensor", None),
        P("tensor", None),
    )
    out_specs = (
        P(("dp", "tensor"), None),
        P(("dp", "tensor"), None),
        P("tensor", "dp", None, None),
        P("tensor", "dp", None, None),
        P("tensor", "dp", None, None),
    )
    return jax.shard_map(local, mesh=mesh, in_specs=in_specs, out_specs=out_specs, check_vma=False)
```

```python
import functools
import math

import jax
import jax.numpy as jnp
from jax import lax
from jax.experimental import pallas as pl
from jax.experimental.pallas import tpu as pltpu
from jax.sharding import PartitionSpec as P

FF = 14336
BF16 = jnp.bfloat16
F32 = jnp.float32
VMEM = pltpu.VMEM
SMEM = pltpu.SMEM


SMEM_SPEC = pl.BlockSpec(memory_space=SMEM)
HBM_SPEC = pl.BlockSpec(memory_space=pltpu.HBM)
ANY_SPEC = pl.BlockSpec(memory_space=pl.ANY)
FREE = pl.CostEstimate(flops=0, bytes_accessed=0, transcendentals=0)
LIMIT = pltpu.CompilerParams(vmem_limit_bytes=4 * 2**20)
DENSE_LIMIT = 17 * 2**20
NEXT_LIMIT = 17 * 2**20


def in_vmem():
    return pl.BlockSpec(memory_space=VMEM)


def pinned(*arrays):
    return [pltpu.with_memory_space_constraint(x, VMEM) for x in arrays]


def in_hbm(x):
    return pltpu.with_memory_space_constraint(x, pltpu.HBM)


def dot_nn(a, b):
    return lax.dot_general(a, b, (((1,), (0,)), ((), ())), preferred_element_type=F32)


def dot_nt(a, b):
    return lax.dot_general(a, b, (((1,), (1,)), ((), ())), preferred_element_type=F32)


def exchange(x, axis, flip):
    count = lax.axis_size(axis)
    return lax.ppermute(x, axis, [(i, i ^ flip) for i in range(count)])


def assemble(pieces, out):
    chunk = 1024

    def step(n, carry):
        cols = pl.ds(pl.multiple_of(n * chunk, chunk), chunk)
        parts = [x[:, cols].astype(F32) for x in pieces]
        out[:, cols] = jnp.concatenate(parts, axis=0).astype(BF16)
        return carry

    lax.fori_loop(0, out.shape[1] // chunk, step, 0)


def pack(pieces, wait_for=()):
    rows = sum(x.shape[0] for x in pieces)
    width = pieces[0].shape[1]

    def body(*refs):
        assemble(refs[: len(pieces)], refs[-1])

    return pl.pallas_call(
        body,
        out_shape=jax.ShapeDtypeStruct((rows, width), BF16),
        in_specs=[in_vmem()] * len(pieces) + [ANY_SPEC] * len(wait_for),
        out_specs=in_vmem(),
        compiler_params=LIMIT,
        cost_estimate=FREE,
        name="pack",
    )(*pieces, *wait_for)


def side_by_side(left, right):
    rows, width = left.shape

    def body(left_ref, right_ref, out, sem):
        copies = [
            pltpu.make_async_copy(left_ref, out.at[:, pl.ds(0, width)], sem.at[0]),
            pltpu.make_async_copy(right_ref, out.at[:, pl.ds(width, width)], sem.at[1]),
        ]
        for copy in copies:
            copy.start()
        for copy in copies:
            copy.wait()

    return pl.pallas_call(
        body,
        out_shape=jax.ShapeDtypeStruct((rows, 2 * width), BF16),
        in_specs=[HBM_SPEC] * 2,
        out_specs=in_vmem(),
        scratch_shapes=[pltpu.SemaphoreType.DMA((2,))],
        compiler_params=LIMIT,
        name="side_by_side",
    )(in_hbm(left), in_hbm(right))


def add_and_cut(parts, sent, pieces):
    rows, width = sent[0].shape
    height = rows // pieces
    count = len(parts)

    def body(*refs):
        outs = refs[2 * count :]
        chunk = 1024
        for m in range(count):

            def step(n, carry):
                cols = pl.ds(pl.multiple_of(n * chunk, chunk), chunk)
                there = pl.ds(pl.multiple_of(m * width + n * chunk, chunk), chunk)
                total = refs[m][:, cols].astype(F32) + refs[count + m][:, cols].astype(F32)
                for i, out in enumerate(outs):
                    out[:, there] = total[i * height : (i + 1) * height].astype(BF16)
                return carry

            lax.fori_loop(0, width // chunk, step, 0)

    out = (jax.ShapeDtypeStruct((height, count * width), BF16),) * pieces
    return pl.pallas_call(
        body,
        out_shape=out,
        in_specs=[in_vmem()] * (2 * count),
        out_specs=(in_vmem(),) * pieces,
        compiler_params=LIMIT,
        cost_estimate=FREE,
        name="add_and_cut",
    )(*parts, *sent)


def scatter(index, blocks, dense, sem, first, count):
    size = blocks.shape[1]
    cols = dense.shape[1] // size
    scale = 2**16 // cols + 1
    for u in range(count):
        k = first + u
        b = index[0, k]
        r = lax.shift_right_logical(b * scale, 16)
        c = b - r * cols
        r, c = pl.multiple_of(r * size, size), pl.multiple_of(c * size, size)
        pltpu.make_async_copy(
            blocks.at[k], dense.at[pl.ds(r, size), pl.ds(c, size)], sem
        ).start()


def dense_body(index_hbm, blocks, *refs):
    dense, index, sem = refs[-3:]
    fetch = pltpu.make_async_copy(index_hbm, index, sem.at[1])
    fetch.start()
    dense[...] = jnp.zeros_like(dense)
    fetch.wait()
    fill_dense(index, blocks, dense, sem.at[0])
    pltpu.make_async_copy(blocks, blocks, sem.at[0]).wait()


def fill_dense(index, blocks, dense, sem):
    kept = blocks.shape[0]
    unroll = 8 if kept % 8 == 0 else 1

    def step(i, carry):
        scatter(index, blocks, dense, sem, i * unroll, unroll)
        return carry

    lax.fori_loop(0, kept // unroll, step, 0)


def dense_first_body(cap, index_hbm, blocks, source, *refs):
    lists, (dense, copied, spots, index, rows, sem) = refs[:6], refs[6:]
    copy = pltpu.make_async_copy(source, copied, sem.at[2])
    copy.start()
    fetch = pltpu.make_async_copy(index_hbm, index, sem.at[1])
    fetch.start()
    for n, ref in enumerate(lists):
        pltpu.make_async_copy(ref, rows.at[n], sem.at[3]).start()
    dense[...] = jnp.zeros_like(dense)
    fetch.wait()
    fill_dense(index, blocks, dense, sem.at[0])
    pltpu.make_async_copy(rows, rows, sem.at[3]).wait()
    kept = rows.shape[2]
    room = spots.shape[1]
    mine = lax.axis_index("dp") * cap + lax.broadcasted_iota(jnp.int32, (room, kept), 0)
    for n in range(3):
        held = jnp.where(rows[n] == mine, rows[3 + n] + 1, 0)
        found = jnp.sum(held, axis=1, keepdims=True) - 1
        spots[n : n + 1] = jnp.broadcast_to(found, (room, 128)).T[:1]
    copy.wait()
    pltpu.make_async_copy(blocks, blocks, sem.at[0]).wait()


def dense_first(index, blocks, source, slots, indexes, cap, width, hidden, limit):
    return pl.pallas_call(
        functools.partial(dense_first_body, cap),
        out_shape=(
            VMEM((width, hidden), BF16),
            VMEM(source.shape, source.dtype),
            jax.ShapeDtypeStruct((3, -(-cap // 128) * 128), jnp.int32),
        ),
        in_specs=[HBM_SPEC] * 2 + [ANY_SPEC] + [HBM_SPEC] * 6,
        out_specs=(in_vmem(),) * 3,
        scratch_shapes=[
            pltpu.SMEM(index.shape, jnp.int32),
            VMEM((6, *index.shape), jnp.int32),
            pltpu.SemaphoreType.DMA((4,)),
        ],
        compiler_params=pltpu.CompilerParams(vmem_limit_bytes=limit),
        cost_estimate=FREE,
        name="dense_first",
    )(in_hbm(index), in_hbm(blocks), source, *(in_hbm(x) for x in (*slots, *indexes)))


def dense(index, blocks, width, hidden, limit, wait_for):
    return pl.pallas_call(
        dense_body,
        out_shape=VMEM((width, hidden), BF16),
        in_specs=[HBM_SPEC] * 2 + [ANY_SPEC] * len(wait_for),
        out_specs=in_vmem(),
        scratch_shapes=[pltpu.SMEM(index.shape, jnp.int32), pltpu.SemaphoreType.DMA((2,))],
        compiler_params=pltpu.CompilerParams(vmem_limit_bytes=limit),
        cost_estimate=FREE,
        name="dense",
    )(in_hbm(index), in_hbm(blocks), *wait_for)


def chunk_of(hidden):
    return 256 if hidden % 256 == 0 else 128


def broad_of(hidden):
    return 896 if hidden % 896 == 0 else 128


def acts_body(count, *refs):
    pieces, (wg, wu, wd_hbm), refs = refs[:count], refs[count : count + 3], refs[count + 3 :]
    hid, gp, up, x, wd, sem = refs[-6:]
    width, hidden = wg.shape
    chunk = wd.shape[1]
    steps = hidden // chunk

    def place(n):
        return pl.ds(pl.multiple_of(n * chunk, chunk), chunk)

    def fetch(n):
        slot = lax.rem(n, 2)
        return pltpu.make_async_copy(wd_hbm.at[place(n)], wd.at[slot], sem.at[slot])

    fetch(0).start()
    assemble(pieces, x)

    def step(n, carry):
        @pl.when(n + 1 < steps)
        def _():
            fetch(n + 1).start()

        cols = place(n)
        g = dot_nn(x[:, :width], wg[:, cols])
        u = dot_nn(x[:, :width], wu[:, cols])
        fetch(n).wait()
        h = dot_nt(x[:, width:], wd[lax.rem(n, 2)])
        s = jax.nn.sigmoid(g)
        hid[:, cols] = (g * s * u).astype(BF16)
        gp[:, cols] = (h * u * s * (1.0 + g * (1.0 - s))).astype(BF16)
        up[:, cols] = (h * g * s).astype(BF16)
        return carry

    lax.fori_loop(0, steps, step, 0)


def acts_pass(pieces, wg, wu, wd, name, wait_for=()):
    rows = sum(x.shape[0] for x in pieces)
    width, hidden = wg.shape
    chunk = chunk_of(hidden)
    act = VMEM((rows, hidden), BF16)
    need = 84 * rows * chunk + 4 * chunk * width + 2**20 + (rows > 256) * 18 * 2**20
    return pl.pallas_call(
        functools.partial(acts_body, len(pieces)),
        out_shape=(act, act, act, VMEM((rows, 2 * width), BF16)),
        in_specs=[in_vmem()] * (len(pieces) + 2) + [HBM_SPEC] + [ANY_SPEC] * len(wait_for),
        out_specs=(in_vmem(),) * 4,
        scratch_shapes=[VMEM((2, chunk, width), BF16), pltpu.SemaphoreType.DMA((2,))],
        compiler_params=pltpu.CompilerParams(vmem_limit_bytes=max(need, 8 * 2**20)),
        cost_estimate=pl.CostEstimate(
            flops=6 * rows * width * hidden, bytes_accessed=2 * width * hidden, transcendentals=0
        ),
        name=name,
    )(*pieces, *pinned(wg, wu), in_hbm(wd), *wait_for)


def own_body(count, index_hbm, *refs):
    pieces, (wg, wu, blocks), refs = refs[:count], refs[count : count + 3], refs[count + 3 :]
    hid, gp, up, x, part, back, wd_out, wd, g_all, u_all, index, sem = refs
    width, hidden = wg.shape
    chunk = broad_of(hidden)
    steps = hidden // chunk
    fetch = pltpu.make_async_copy(index_hbm, index, sem.at[1])
    fetch.start()
    assemble(pieces, x)

    def place(n):
        return pl.ds(pl.multiple_of(n * chunk, chunk), chunk)

    broad = broad_of(hidden)

    def span(n):
        return pl.ds(pl.multiple_of(n * broad, 128), broad)

    def gate(n, carry):
        g_all[:, span(n)] = dot_nn(x[:, :width], wg[:, span(n)])
        wd[span(n)] = jnp.zeros((broad, width), BF16)
        return carry

    lax.fori_loop(0, hidden // broad, gate, 0)
    fetch.wait()
    fill_dense(index, blocks, wd, sem.at[0])

    def up_proj(n, carry):
        u_all[:, span(n)] = dot_nn(x[:, :width], wu[:, span(n)])
        return carry

    lax.fori_loop(0, hidden // broad, up_proj, 0)
    pltpu.make_async_copy(blocks, blocks, sem.at[0]).wait()
    store = pltpu.make_async_copy(wd, wd_out, sem.at[2])
    store.start()

    def grad(n, carry):
        cols = place(n)
        g, u = g_all[:, cols], u_all[:, cols]
        h = dot_nt(x[:, width:], wd[cols])
        s = jax.nn.sigmoid(g)
        hid[:, cols] = (g * s * u).astype(BF16)
        gp[:, cols] = (h * u * s * (1.0 + g * (1.0 - s))).astype(BF16)
        up[:, cols] = (h * g * s).astype(BF16)
        return carry

    lax.fori_loop(0, steps, grad, 0)
    half = part.shape[0]
    wide = 2048

    def sums(n, carry):
        out = pl.ds(pl.multiple_of(n * wide, wide), wide)
        later = pl.ds(pl.multiple_of(width + n * wide, wide), wide)
        left = dot_nn(hid[...], wd[:, out]).astype(BF16)
        right = (dot_nt(gp[...], wg[out, :]) + dot_nt(up[...], wu[out, :])).astype(BF16)
        part[:, out] = left[:half]
        back[:, out] = left[half:]
        part[:, later] = right[:half]
        back[:, later] = right[half:]
        return carry

    lax.fori_loop(0, width // wide, sums, 0)
    store.wait()


def own_pass(pieces, wg, wu, index, blocks, limit):
    rows = sum(x.shape[0] for x in pieces)
    width, hidden = wg.shape
    act = VMEM((rows, hidden), BF16)
    half = VMEM((rows // 2, 2 * width), BF16)
    kept = VMEM((rows, hidden), F32)
    return pl.pallas_call(
        functools.partial(own_body, len(pieces)),
        out_shape=(
            act, act, act, VMEM((rows, 2 * width), BF16), half, half,
            pltpu.HBM((hidden, width), BF16),
        ),
        in_specs=[HBM_SPEC] + [in_vmem()] * (len(pieces) + 2) + [HBM_SPEC],
        out_specs=(in_vmem(),) * 6 + (HBM_SPEC,),
        scratch_shapes=[
            VMEM((hidden, width), BF16),
            kept,
            kept,
            pltpu.SMEM(index.shape, jnp.int32),
            pltpu.SemaphoreType.DMA((3,)),
        ],
        compiler_params=pltpu.CompilerParams(vmem_limit_bytes=limit),
        cost_estimate=pl.CostEstimate(
            flops=12 * rows * width * hidden, bytes_accessed=2 * width * hidden, transcendentals=0
        ),
        name="own_pass",
    )(in_hbm(index), *pieces, *pinned(wg, wu), in_hbm(blocks))


def grads_body(
    factor, size, group, spots, own, rest, hid0, hid1, gp0, gp1, up0, up1, *refs
):
    sums = refs[:-11]
    layer, token_grad, gate_out, up_out, down_out = refs[-11:-6]
    tok_t, hid_t, gate_buf, up_buf, down_buf, sem = refs[-6:]
    cap = gate_buf.shape[0]
    groups = cap // group
    d_cols = tok_t.shape[0]
    ff_cols = hid_t.shape[0]
    width = d_cols * size

    def column(first, second, start):
        cols = pl.ds(pl.multiple_of(start, size), size)
        return jnp.concatenate([first[:, cols], second[:, cols]], axis=0)

    def one(which, left, first, second, base, buf, cols, slot):
        spot = spots[which, slot]
        b = jnp.maximum(spot, 0)
        r = lax.shift_right_logical(b * (2**16 // cols + 1), 16)
        c = b - r * cols
        value = dot_nn(left[r], column(first, second, base + c * size)) * factor
        buf[slot] = jnp.where(spot >= 0, value, 0.0)

    def send(buf, out, slot, i):
        part = pl.ds(i * group, group)
        pltpu.make_async_copy(buf.at[part], out.at[part], sem.at[slot]).start()

    def last_sum(n, carry):
        chunk = 1024
        for out, base in ((layer, 0), (token_grad, width)):
            cols = pl.ds(pl.multiple_of(n * chunk, chunk), chunk)
            there = pl.ds(pl.multiple_of(base + n * chunk, chunk), chunk)
            total = sums[0][:, there].astype(F32)
            for piece in sums[1:]:
                total = total + piece[:, there].astype(F32)
            out[:, cols] = total.astype(BF16)
        return carry

    lax.fori_loop(0, width // 1024, last_sum, 0)

    def turn_hidden(n, carry):
        hid_t[n] = column(hid0, hid1, n * size).T
        return carry

    lax.fori_loop(0, ff_cols, turn_hidden, 0)
    turns = -(-d_cols // groups)

    def down_step(i, carry):
        for j in range(max(group, turns)):
            if j < turns:
                n = jnp.minimum(i * turns + j, d_cols - 1)
                tok_t[n] = column(own, rest, n * size).T
            if j < group:
                one(2, hid_t, own, rest, width, down_buf, d_cols, i * group + j)
        send(down_buf, down_out, 2, i)
        return carry

    lax.fori_loop(0, groups, down_step, 0)

    def step(i, carry):
        for j in range(group):
            one(0, tok_t, gp0, gp1, 0, gate_buf, ff_cols, i * group + j)
            one(1, tok_t, up0, up1, 0, up_buf, ff_cols, i * group + j)
        send(gate_buf, gate_out, 0, i)
        send(up_buf, up_out, 1, i)
        return carry

    lax.fori_loop(0, groups, step, 0)
    for slot, (buf, out) in enumerate(((gate_buf, gate_out), (up_buf, up_out), (down_buf, down_out))):
        pltpu.make_async_copy(buf, out, sem.at[slot]).wait()


def grads(spots, own, rest, acts0, acts1, sums, size, cap, factor):
    group = max(n for n in range(1, 18) if cap % n == 0)
    width = own.shape[1] // 2
    hidden = acts0[0].shape[1]
    rows = own.shape[0] + rest.shape[0]
    out = jax.ShapeDtypeStruct((cap, size, size), F32)
    buf = VMEM((cap, size, size), F32)
    need = rows * (6 * width + 8 * hidden) + cap * 12 * size * size
    return pl.pallas_call(
        functools.partial(grads_body, factor, size, group),
        out_shape=(jax.ShapeDtypeStruct((sums[0].shape[0], width), BF16),) * 2 + (out, out, out),
        in_specs=[SMEM_SPEC] + [in_vmem()] * (8 + len(sums)),
        out_specs=(in_vmem(),) * 2 + (HBM_SPEC,) * 3,
        scratch_shapes=[
            VMEM((width // size, size, rows), BF16),
            VMEM((hidden // size, size, rows), BF16),
            buf,
            buf,
            buf,
            pltpu.SemaphoreType.DMA((3,)),
        ],
        compiler_params=pltpu.CompilerParams(vmem_limit_bytes=need + 2**21),
        cost_estimate=pl.CostEstimate(
            flops=6 * cap * size * size * rows, bytes_accessed=12 * cap * size * size, transcendentals=0
        ),
        name="grads",
    )(spots, own, rest, acts0[0], acts1[0], acts0[1], acts1[1], acts0[2], acts1[2], *sums)


def local(
    tokens,
    out_grad,
    gate_blocks,
    up_blocks,
    down_blocks,
    gate_index,
    up_index,
    down_index,
    gate_slot,
    up_slot,
    down_slot,
):
    rows, width = tokens.shape
    size = gate_blocks.shape[1]
    kept_count = gate_blocks.shape[0]
    groups = lax.axis_size("dp")
    slices = lax.axis_size("tensor")
    hidden = FF // slices
    cap = (kept_count + groups - 1) // groups + kept_count // (4 * groups)
    factor = 1.0 / math.sqrt(rows * slices * groups)

    both = side_by_side(tokens, out_grad)
    chips = range(2, slices, 2)

    def sibling(x):
        return exchange(x, "tensor", 1)

    far = [exchange(both, "dp", a) for a in range(1, groups)]
    near = [exchange(both, "tensor", d) for d in chips[:-1]]
    stage = 2 * width * hidden
    wu, later, spots = dense_first(
        up_index,
        up_blocks,
        both,
        (gate_slot, up_slot, down_slot),
        (gate_index, up_index, down_index),
        cap,
        width,
        hidden,
        DENSE_LIMIT,
    )
    near.append(exchange(later, "tensor", chips[-1]))
    others = pack(far, [wu])
    wg = dense(gate_index, gate_blocks, width, hidden, NEXT_LIMIT, [others])
    own_half = pack([both, *near], [wg])
    own_pieces = [own_half, sibling(own_half)]
    other_half = [others, *(exchange(others, "tensor", d) for d in chips)]

    *acts0, own, part, back, wd = own_pass(
        own_pieces, wg, wu, down_index, down_blocks, stage + 3 * 2**20
    )
    chip = add_and_cut([part], [sibling(back)], slices // 2)
    acts1_in = [*other_half, *(sibling(x) for x in other_half)]
    *acts1, rest = acts_pass(acts1_in, wg, wu, wd, "rest_acts", [chip[0]])

    sums = [chip[0], *(exchange(piece, "tensor", d) for piece, d in zip(chip[1:], chips))]
    layer_out, token_grad, gate_out, up_out, down_out = grads(
        spots, own, rest, acts0, acts1, sums, size, cap, factor
    )
    return (layer_out, token_grad, gate_out[None], up_out[None], down_out[None])


def solution(mesh):
    in_specs = (
        P(("dp", "tensor"), None),
        P(("dp", "tensor"), None),
        P("tensor", None, None),
        P("tensor", None, None),
        P("tensor", None, None),
        P("tensor", None),
        P("tensor", None),
        P("tensor", None),
        P("tensor", None),
        P("tensor", None),
        P("tensor", None),
    )
    out_specs = (
        P(("dp", "tensor"), None),
        P(("dp", "tensor"), None),
        P("tensor", "dp", None, None),
        P("tensor", "dp", None, None),
        P("tensor", "dp", None, None),
    )
    return jax.shard_map(local, mesh=mesh, in_specs=in_specs, out_specs=out_specs, check_vma=False)
```
